32 devices in a mesh: seq: 8 (over z, x), tp: 4 (over y, core).
Axes of the slice: x: 2, y: 2, z: 4, core: 2. Of those that a mesh axis runs over, the one named last changes fastest.
Arguments:
- teacher_hidden: bfloat16 [1024, 4096], P('seq', 'tp'), may hold values from -6 to 6
- proj_weight: bfloat16 [4096, 3584], P('tp'), may hold values from -0.09375 to 0.09375
- student_in: bfloat16 [1280, 3584], P('seq'), may hold values from -6 to 6
- norm_gain: float32 [3584], replicated, may hold values from 0.25 to 1.75
- w_query: bfloat16 [3584, 1024], P(None, 'tp')
- w_keyval: bfloat16 [3584, 1024], P(None, 'tp')
- w_out: bfloat16 [1024, 3584], P('tp'), may hold values from -0.1875 to 0.1875
- row_offsets: int32 [8], P('seq'), may hold values from 0 to 864, as said below
- row_counts: int32 [8], P('seq'), may hold values from 96 to 160, as said below
- doc_start: int32 [1280], P('seq'), may hold values from 0 to 159, as said below
Outputs:
- student_out: bfloat16 [1280, 3584], P('seq')
- grad_in: bfloat16 [1280, 3584], P(('seq', 'tp'))
The draws below stay inside these ranges and needn't reach their ends.
Inputs may be any that keep to these rules, and one draw needn't show every extreme that they name: Block s holds the tokens row_offsets[s] to row_offsets[s] + row_counts[s] - 1 in its first slots; row_offsets[0] = 0, for s >= 1 row_offsets[s] lies between s * 128 - 128 // 4 and s * 128 - 1, and row_offsets[s] + row_counts[s] = row_offsets[s + 1], the last block ending at 1024. `row_counts`: see row_offsets; some block holds 160 tokens and some 128 - 128 // 4. Within a block doc_start never falls, doc_start[p] <= p, documents lie whole in one block, and the slots from row_counts onward start a new document at row_counts.
All inputs are finite; a program needn't handle non-finite values.
Results may differ from the reference program's by a relative error of at most 0.028.
The reference program's roundings to bfloat16 on the way count: a program that leaves them out, or rounds other values in their place, can miss the bound.
Values may be sent and summed in bfloat16 or wider, within the bound.
A program may use at most 64 MiB of HBM per device.

```python
import math
import jax
import jax.numpy as jnp
from jax import lax

DT = 4096
DS = 3584
HD = 128
QPK = 2
DOC_MEAN = 64
TOK_DEV = 128
SCAP = 160
KVH = 4
HQ = 8
TOKENS = 1024
SROWS = 1280
N_SEQ = 8
N_TP = 4


def layout_plan(key):
    first = jax.random.fold_in(key, 11)
    third = jax.random.fold_in(key, 13)
    quarter = TOK_DEV // 4
    index = jnp.arange(N_SEQ, dtype=jnp.int32)
    delta = jax.random.randint(first, (N_SEQ,), -quarter, 0)
    delta = jnp.where((index == 1) | (index == N_SEQ - 1), -quarter, delta)
    delta = jnp.where(index == 0, 0, delta)
    offsets = index * TOK_DEV + delta
    ends = jnp.concatenate([offsets[1:], jnp.full((1,), N_SEQ * TOK_DEV, jnp.int32)])
    counts = ends - offsets
    slots = jnp.arange(SCAP, dtype=jnp.int32)[None, :]
    flags = (jax.random.randint(third, (N_SEQ, SCAP), 0, DOC_MEAN) == 0) | (slots == 0) | (slots == counts[:, None])
    starts = lax.cummax(jnp.where(flags, slots, 0), axis=1)
    return (offsets.astype(jnp.int32), counts.astype(jnp.int32), starts.reshape(SROWS).astype(jnp.int32))


def attention_weights(key):
    qkey = jax.random.fold_in(key, 21)
    kkey = jax.random.fold_in(key, 22)
    wq = jax.random.normal(qkey, (DS, KVH, QPK, HD), jnp.float32) / math.sqrt(DS)
    wkv = jax.random.normal(kkey, (DS, KVH, 2, HD), jnp.float32) / math.sqrt(DS)
    return (wq.reshape(DS, HQ * HD).astype(jnp.bfloat16), wkv.reshape(DS, KVH * 2 * HD).astype(jnp.bfloat16))


def draw_w_query(key, part):
    return attention_weights(key)[0]


def draw_w_keyval(key, part):
    return attention_weights(key)[1]


def draw_row_offsets(key, part):
    return layout_plan(key)[0]


def draw_row_counts(key, part):
    return layout_plan(key)[1]


def draw_doc_start(key, part):
    return layout_plan(key)[2]


def level_of(own_key, extent, split, low, largest):
    def one(dim, shards_of):
        heights = jax.random.uniform(jax.random.fold_in(jax.random.fold_in(own_key, 6), dim), (shards_of,), jnp.float32, low / len(split), largest / len(split))
        return jnp.repeat(jnp.exp(heights), extent[dim] // shards_of).reshape((-1,) + (1,) * (len(extent) - dim - 1))

    gain = one(*split[0])
    for cut in split[1:]:
        gain = gain * one(*cut)
    return gain


def bell_draw(rng, shape, scale, limit, pieces=(), held_as=jnp.bfloat16):
    loudness = level_of(rng, shape, pieces, -0.22, 0.18) if pieces else 1.0
    result = jax.random.normal(rng, shape, jnp.float32) * scale * loudness
    return jnp.minimum(jnp.maximum(result, -limit), limit).astype(held_as)


def setup_inputs(seed: int = 0) -> dict:
    key_of = jax.random.split(jax.random.key(seed), 11)
    teacher_hidden = bell_draw(key_of[0], (TOKENS, DT), 1.0, 6.0, ((0, 8), (1, 4)))
    proj_weight = bell_draw(key_of[1], (DT, DS), DT ** -0.5, 0.09375, ((0, 4),))
    student_in = bell_draw(key_of[2], (SROWS, DS), 1.0, 6.0, ((0, 8),))
    norm_gain = jnp.clip(1.0 + 0.15 * jax.random.normal(key_of[3], (DS,), jnp.float32), 0.25, 1.75)
    w_query = draw_w_query(jax.random.fold_in(key_of[10], 71), 0)
    w_keyval = draw_w_keyval(jax.random.fold_in(key_of[10], 71), 0)
    w_out = bell_draw(key_of[6], (HQ * HD, DS), (HQ * HD) ** -0.5, 0.1875, ((0, 4),))
    row_offsets = draw_row_offsets(jax.random.fold_in(key_of[10], 71), 0)
    row_counts = draw_row_counts(jax.random.fold_in(key_of[10], 71), 0)
    doc_start = draw_doc_start(jax.random.fold_in(key_of[10], 71), 0)
    return {"teacher_hidden": teacher_hidden, "proj_weight": proj_weight, "student_in": student_in, "norm_gain": norm_gain, "w_query": w_query, "w_keyval": w_keyval, "w_out": w_out, "row_offsets": row_offsets, "row_counts": row_counts, "doc_start": doc_start}


epsilon = 1e-06

def student_block(rows, goal, count, starts, norm_gain, w_query, w_keyval, w_out):
    scale = 1.0 / math.sqrt(HD)
    xf = rows.astype(jnp.float32)
    inv = lax.rsqrt(lax.optimization_barrier(jnp.mean(xf * xf, axis=1, keepdims=True)) + epsilon)
    normed = (xf * inv * norm_gain).astype(jnp.bfloat16)
    query = jnp.dot(normed, w_query, preferred_element_type=jnp.float32).astype(jnp.bfloat16)
    keyval = jnp.dot(normed, w_keyval, preferred_element_type=jnp.float32).astype(jnp.bfloat16)
    qheads = query.reshape(SCAP, KVH, QPK, HD).astype(jnp.float32)
    kvheads = keyval.reshape(SCAP, KVH, 2, HD).astype(jnp.float32)
    keys = kvheads[:, :, 0, :]
    values = kvheads[:, :, 1, :]
    slots = jnp.arange(SCAP, dtype=jnp.int32)
    allowed = (slots[None, :] >= starts[:, None]) & (slots[None, :] <= slots[:, None])
    scores = jnp.einsum('pgeh,kgh->gepk', qheads, keys) * scale
    scores = jnp.where(allowed[None, None], scores, -jnp.inf)
    top = lax.optimization_barrier(jnp.max(scores, axis=-1, keepdims=True))
    expo = jnp.exp(scores - top)
    probs = expo / lax.optimization_barrier(jnp.sum(expo, axis=-1, keepdims=True))
    probs_b = probs.astype(jnp.bfloat16).astype(jnp.float32)
    attn = jnp.einsum('gepk,kgh->pgeh', probs_b, values).astype(jnp.bfloat16)
    attn = attn.reshape(SCAP, HQ * HD)
    width = QPK * HD
    branch = jnp.zeros((SCAP, DS), jnp.float32)
    for j in range(N_TP):
        piece = jnp.dot(attn[:, j * width:(j + 1) * width], w_out[j * width:(j + 1) * width], preferred_element_type=jnp.float32)
        branch = branch + piece.astype(jnp.bfloat16).astype(jnp.float32)
    student_out = (xf + branch).astype(jnp.bfloat16)
    yf = student_out.astype(jnp.float32)
    tf = goal.astype(jnp.float32)
    live = (slots < count).astype(jnp.float32)[:, None]
    asum = lax.optimization_barrier(jnp.sum(yf * yf, axis=1, keepdims=True)) + epsilon
    bsum = lax.optimization_barrier(jnp.sum(tf * tf, axis=1, keepdims=True)) + epsilon
    both = lax.rsqrt(asum * bsum)
    cosv = lax.optimization_barrier(jnp.sum(yf * tf, axis=1, keepdims=True)) * both
    dy = -math.sqrt(DS) * live * (tf * both - cosv * yf / asum)
    dy_b = dy.astype(jnp.bfloat16)
    d_attn = jnp.dot(dy_b, w_out.T, preferred_element_type=jnp.float32).astype(jnp.bfloat16)
    d_out = d_attn.reshape(SCAP, KVH, QPK, HD).astype(jnp.float32)
    d_values = jnp.einsum('gepk,pgeh->kgh', probs_b, d_out).astype(jnp.bfloat16)
    dprob = jnp.einsum('pgeh,kgh->gepk', d_out, values)
    dscore = probs * (dprob - lax.optimization_barrier(jnp.sum(dprob * probs, axis=-1, keepdims=True))) * scale
    dscore_b = dscore.astype(jnp.bfloat16).astype(jnp.float32)
    d_query = jnp.einsum('gepk,kgh->pgeh', dscore_b, keys).astype(jnp.bfloat16).reshape(SCAP, HQ * HD)
    d_keys = jnp.einsum('gepk,pgeh->kgh', dscore_b, qheads).astype(jnp.bfloat16)
    d_keyval = jnp.stack([d_keys, d_values], axis=2).reshape(SCAP, KVH * 2 * HD)
    d_normed = jnp.dot(d_query, w_query.T, preferred_element_type=jnp.float32) + jnp.dot(d_keyval, w_keyval.T, preferred_element_type=jnp.float32)
    upper = d_normed * norm_gain
    dx = inv * upper - xf * inv * inv * inv * lax.optimization_barrier(jnp.mean(upper * xf, axis=1, keepdims=True))
    grad_in = (dy + dx).astype(jnp.bfloat16)
    return (student_out, grad_in)

def reference(teacher_hidden, proj_weight, student_in, norm_gain, w_query, w_keyval, w_out, row_offsets, row_counts, doc_start):
    group = DT // N_TP
    total = jnp.zeros((TOKENS, DS), jnp.float32)
    for j in range(N_TP):
        piece = jnp.dot(teacher_hidden[:, j * group:(j + 1) * group], proj_weight[j * group:(j + 1) * group], preferred_element_type=jnp.float32)
        total = total + piece.astype(jnp.bfloat16).astype(jnp.float32)
    target = jnp.concatenate([total.astype(jnp.bfloat16), jnp.zeros((SCAP, DS), jnp.bfloat16)], axis=0)

    def one_block(index):
        rows = lax.dynamic_slice_in_dim(student_in, index * SCAP, SCAP, 0)
        goal = lax.dynamic_slice_in_dim(target, row_offsets[index].astype(jnp.int32), SCAP, 0)
        starts = lax.dynamic_slice_in_dim(doc_start, index * SCAP, SCAP, 0)
        return student_block(rows, goal, row_counts[index], starts, norm_gain, w_query, w_keyval, w_out)
    outputs, grads = lax.map(one_block, jnp.arange(N_SEQ, dtype=jnp.int32))
    return (outputs.reshape(SROWS, DS), grads.reshape(SROWS, DS))
```

```python
import functools
import math

import jax
import jax.numpy as jnp
from jax import lax
from jax.experimental import pallas as pl
from jax.experimental.pallas import tpu as pltpu
from jax.sharding import PartitionSpec as P

HD = 128
QPK = 2


epsilon = 1e-06


def from_behind(block, axis, distance):
    devices = range(lax.axis_size(axis))
    route = [(i - distance, i) for i in devices if i - distance in devices]
    return lax.ppermute(block, axis, route)


def plain_body(
    teacher_hidden,
    proj_weight,
    student_in,
    norm_gain,
    w_query,
    w_keyval,
    w_out,
    row_offsets,
    row_counts,
    doc_start,
):
    scale = 1.0 / math.sqrt(HD)
    tokens_here = teacher_hidden.shape[0]
    quarter = tokens_here // 4
    slots_here = student_in.shape[0]
    width = student_in.shape[1]
    start = row_offsets[0] - lax.axis_index("seq") * tokens_here + quarter
    count = row_counts[0]
    xf = student_in.astype(jnp.float32)
    inv = lax.rsqrt(jnp.mean(xf * xf, axis=1, keepdims=True) + epsilon)
    normed = (xf * inv * norm_gain).astype(jnp.bfloat16)
    query = (
        jnp.dot(normed, w_query, preferred_element_type=jnp.float32)
        .astype(jnp.bfloat16)
        .reshape(slots_here, QPK, HD)
    )
    keyval = (
        jnp.dot(normed, w_keyval, preferred_element_type=jnp.float32)
        .astype(jnp.bfloat16)
        .reshape(slots_here, 2, HD)
    )
    keys = keyval[:, 0, :]
    values = keyval[:, 1, :]
    slots = jnp.arange(slots_here, dtype=jnp.int32)
    allowed = (slots[None, :] >= doc_start[:, None]) & (slots[None, :] <= slots[:, None])
    scores = jnp.einsum("peh,kh->epk", query, keys, preferred_element_type=jnp.float32) * scale
    scores = jnp.where(allowed[None], scores, -jnp.inf)
    top = jnp.max(scores, axis=-1, keepdims=True)
    expo = jnp.exp(scores - top)
    probs = expo / jnp.sum(expo, axis=-1, keepdims=True)
    probs_b = probs.astype(jnp.bfloat16)
    attn = jnp.einsum("epk,kh->peh", probs_b, values, preferred_element_type=jnp.float32).astype(
        jnp.bfloat16
    )
    attn = attn.reshape(slots_here, QPK * HD)
    branch_part = jnp.dot(attn, w_out, preferred_element_type=jnp.float32).astype(jnp.bfloat16)
    earlier = from_behind(teacher_hidden[tokens_here - quarter :], "seq", 1)
    features = jnp.concatenate(
        [earlier, teacher_hidden, jnp.zeros((quarter, teacher_hidden.shape[1]), jnp.bfloat16)],
        axis=0,
    )
    picked = lax.dynamic_slice_in_dim(features, start, slots_here, 0)
    projected = jnp.dot(picked, proj_weight, preferred_element_type=jnp.float32).astype(
        jnp.bfloat16
    )
    goal_sum, branch = (
        lax.psum(projected, "tp").astype(jnp.float32),
        lax.psum(branch_part, "tp").astype(jnp.float32),
    )
    goal = goal_sum.astype(jnp.bfloat16)
    student_out = (xf + branch).astype(jnp.bfloat16)
    yf = student_out.astype(jnp.float32)
    tf = goal.astype(jnp.float32)
    live = (slots < count).astype(jnp.float32)[:, None]
    asum = jnp.sum(yf * yf, axis=1, keepdims=True) + epsilon
    bsum = jnp.sum(tf * tf, axis=1, keepdims=True) + epsilon
    both = lax.rsqrt(asum * bsum)
    cosv = jnp.sum(yf * tf, axis=1, keepdims=True) * both
    dy = -math.sqrt(width) * live * (tf * both - cosv * yf / asum)
    dy_b = dy.astype(jnp.bfloat16)
    d_attn = lax.dot_general(
        dy_b, w_out, (((1,), (1,)), ((), ())), preferred_element_type=jnp.float32
    ).astype(jnp.bfloat16)
    d_out = d_attn.reshape(slots_here, QPK, HD)
    d_values = jnp.einsum("epk,peh->kh", probs_b, d_out, preferred_element_type=jnp.float32).astype(
        jnp.bfloat16
    )
    dprob = jnp.einsum("peh,kh->epk", d_out, values, preferred_element_type=jnp.float32)
    dscore = probs * (dprob - jnp.sum(dprob * probs, axis=-1, keepdims=True)) * scale
    dscore_b = dscore.astype(jnp.bfloat16)
    d_query = jnp.einsum("epk,kh->peh", dscore_b, keys, preferred_element_type=jnp.float32).astype(
        jnp.bfloat16
    )
    d_query = d_query.reshape(slots_here, QPK * HD)
    d_keys = jnp.einsum("epk,peh->kh", dscore_b, query, preferred_element_type=jnp.float32).astype(
        jnp.bfloat16
    )
    d_keyval = jnp.stack([d_keys, d_values], axis=1).reshape(slots_here, 2 * HD)
    own_rows = slots_here // lax.axis_size("tp")
    total = lax.dot_general(
        d_query, w_query, (((1,), (1,)), ((), ())), preferred_element_type=jnp.float32
    )
    d_normed = lax.psum_scatter(
        (
            total
            + lax.dot_general(
                d_keyval, w_keyval, (((1,), (1,)), ((), ())), preferred_element_type=jnp.float32
            )
        ).astype(jnp.bfloat16),
        "tp",
        scatter_dimension=0,
        tiled=True,
    ).astype(jnp.float32)
    first_row = lax.axis_index("tp") * own_rows
    x_own = lax.dynamic_slice_in_dim(xf, first_row, own_rows, 0)
    inv_own = lax.dynamic_slice_in_dim(inv, first_row, own_rows, 0)
    dy_own = lax.dynamic_slice_in_dim(dy, first_row, own_rows, 0)
    upper = d_normed * norm_gain
    dx = inv_own * upper - x_own * inv_own * inv_own * inv_own * jnp.mean(
        upper * x_own, axis=1, keepdims=True
    )
    grad_in = (dy_own + dx).astype(jnp.bfloat16)
    return (student_out, grad_in)


MESH = pl.DeviceIdType.MESH
NT = (((1,), (1,)), ((), ()))
TN = (((0,), (0,)), ((), ()))
F32 = jnp.float32
BF16 = jnp.bfloat16


def dot(a, b, dims=None):
    if dims is None:
        return jnp.dot(a, b, preferred_element_type=F32)
    return lax.dot_general(a, b, dims, preferred_element_type=F32)


def step_kernel(
    n_seq,
    offset_ref,
    count_ref,
    start_ref,
    gain_ref,
    teacher_hbm,
    proj_hbm,
    x_hbm,
    wq_hbm,
    wkv_hbm,
    wo_hbm,
    out_ref,
    grad_ref,
    feat,
    proj,
    x_in,
    wq,
    wkv,
    wo,
    xq,
    normed,
    inv_s,
    qkv,
    probs_s,
    attn_s,
    g_part,
    g_near,
    g_chip,
    g_far,
    b_part,
    b_near,
    b_chip,
    b_far,
    t_s,
    y_s,
    dy_s,
    dy_own,
    d_attn_s,
    dd_s,
    n_part,
    n_near,
    n_chip,
    n_far,
    dn_s,
    load_sem,
    proj_sem,
    send_sem,
    recv_sem,
    shift_sem,
):
    rows, width = x_in.shape
    quarter = rows // 4
    chunks, _, chunk = proj.shape
    own_tokens = teacher_hbm.shape[0]
    shift = rows - own_tokens
    s = lax.axis_index("seq")
    me = lax.axis_index("tp")
    c = lax.rem(me, 2)
    y = me // 2
    near = {"tp": y * 2 + 1 - c}
    far = {"tp": (1 - y) * 2 + c}
    scale = 1.0 / math.sqrt(HD)

    def cols(k):
        return pl.ds(pl.multiple_of(k * chunk, chunk), chunk)

    loads = [
        pltpu.make_async_copy(a, b, load_sem.at[i])
        for i, (a, b) in enumerate(
            [
                (x_hbm, x_in),
                (wq_hbm, wq),
                (wkv_hbm, wkv),
                (teacher_hbm, feat.at[pl.ds(shift, own_tokens)]),
                (wo_hbm, wo),
            ]
        )
    ]
    for one in loads[:4]:
        one.start()

    def proj_load(k):
        return pltpu.make_async_copy(proj_hbm.at[:, cols(k)], proj.at[k], proj_sem.at[k])

    def start_proj(k, _):
        proj_load(k).start()
        return 0

    lax.fori_loop(0, chunks, start_proj, 0)
    loads[4].start()

    barrier = pltpu.get_barrier_semaphore()
    pl.semaphore_signal(barrier, inc=1, device_id=near, device_id_type=MESH)
    pl.semaphore_signal(barrier, inc=1, device_id=far, device_id_type=MESH)

    @pl.when(s > 0)
    def _():
        pl.semaphore_signal(barrier, inc=1, device_id={"seq": s - 1}, device_id_type=MESH)

    @pl.when(s < n_seq - 1)
    def _():
        pl.semaphore_signal(barrier, inc=1, device_id={"seq": s + 1}, device_id_type=MESH)

    inner = (s > 0) & (s < n_seq - 1)

    @pl.when(inner)
    def _():
        pl.semaphore_wait(barrier, 4)

    @pl.when(jnp.logical_not(inner))
    def _():
        pl.semaphore_wait(barrier, 3)

    def shift_copy(to):
        return pltpu.make_async_remote_copy(
            src_ref=teacher_hbm.at[pl.ds(own_tokens - shift, shift)],
            dst_ref=feat.at[pl.ds(0, shift)],
            send_sem=shift_sem.at[0],
            recv_sem=shift_sem.at[1],
            device_id={"seq": to},
            device_id_type=MESH,
        )

    @pl.when(s < n_seq - 1)
    def _():
        shift_copy(s + 1).start()

    @pl.when(s == 0)
    def _():
        feat[0:shift, :] = jnp.zeros((shift, feat.shape[1]), BF16)

    def remote(kind, k, src, dst, to):
        return pltpu.make_async_remote_copy(
            src_ref=src,
            dst_ref=dst,
            send_sem=send_sem.at[kind, k],
            recv_sem=recv_sem.at[kind, k],
            device_id=to,
            device_id_type=MESH,
        )

    def split_store(ref, k, val):
        for q in range(4):
            ref[k, q % 2, q // 2] = val[q * quarter : (q + 1) * quarter].astype(BF16)

    loads[0].wait()

    def square(k, acc):
        v = x_in[:, cols(k)].astype(F32)
        for q in range(4):
            xq[q % 2, q // 2, :, cols(k)] = v[q * quarter : (q + 1) * quarter]
        return acc + jnp.sum(v * v, axis=1, keepdims=True)

    total = lax.fori_loop(0, chunks, square, jnp.zeros((rows, 1), F32))
    inv = lax.rsqrt(total / width + epsilon)
    for q in range(4):
        inv_s[q] = inv[q * quarter : (q + 1) * quarter]

    def norm(k, _):
        v = x_in[:, cols(k)].astype(F32)
        normed[:, cols(k)] = (v * inv * gain_ref[:, cols(k)]).astype(BF16)
        return 0

    lax.fori_loop(0, chunks, norm, 0)

    start = offset_ref[0] - s * own_tokens + shift
    r_i = lax.broadcasted_iota(jnp.int32, (rows, rows), 0)
    c_i = lax.broadcasted_iota(jnp.int32, (rows, rows), 1)

    @pl.when(s > 0)
    def _():
        shift_copy(s).wait_recv()

    loads[3].wait()
    select = jnp.where(c_i == r_i + start, 1.0, 0.0).astype(BF16)
    feat[...] = dot(select, feat[...]).astype(BF16)

    def near_copy(kind, k, part, land):
        return remote(kind, k, part.at[k, 1 - c], land.at[k], near)

    def far_copy(kind, k, chip, land):
        return remote(kind, k, chip.at[k], land.at[k], far)

    def pass_on(kind, k, part, land, chip, far_land):
        near_copy(kind, k, part, land).wait_recv()
        chip[k] = (part[k, c].astype(F32) + land[k].astype(F32)).astype(BF16)
        far_copy(kind + 1, k, chip, far_land).start()

    def goal_step(k, _):
        proj_load(k).wait()
        split_store(g_part, k, dot(feat[...], proj[k]))
        near_copy(0, k, g_part, g_near).start()

        @pl.when(k > 0)
        def _():
            pass_on(0, k - 1, g_part, g_near, g_chip, g_far)

        return 0

    lax.fori_loop(0, chunks, goal_step, 0)

    loads[1].wait()
    loads[2].wait()
    qkv[:, 0 : QPK * HD] = dot(normed[...], wq[...]).astype(BF16)
    pass_on(0, chunks - 1, g_part, g_near, g_chip, g_far)
    qkv[:, QPK * HD :] = dot(normed[...], wkv[...]).astype(BF16)

    starts = jnp.sum(
        jnp.where(r_i == c_i, start_ref[...].astype(F32), 0.0), axis=1, keepdims=True
    )
    c_f = c_i.astype(F32)
    allowed = (c_f >= starts) & (c_i <= r_i)
    keys = qkv[:, QPK * HD : (QPK + 1) * HD]
    values = qkv[:, (QPK + 1) * HD :]
    for e in range(QPK):
        scores = dot(qkv[:, e * HD : (e + 1) * HD], keys, NT) * scale
        scores = jnp.where(allowed, scores, -jnp.inf)
        expo = jnp.exp(scores - jnp.max(scores, axis=-1, keepdims=True))
        probs = expo / jnp.sum(expo, axis=-1, keepdims=True)
        probs_s[e] = probs
        attn_s[:, e * HD : (e + 1) * HD] = dot(probs.astype(BF16), values).astype(BF16)

    loads[4].wait()

    def branch_step(k, _):
        split_store(b_part, k, dot(attn_s[...], wo[:, cols(k)]))
        near_copy(2, k, b_part, b_near).start()

        @pl.when(k > 0)
        def _():
            pass_on(2, k - 1, b_part, b_near, b_chip, b_far)

        return 0

    lax.fori_loop(0, chunks, branch_step, 0)
    pass_on(2, chunks - 1, b_part, b_near, b_chip, b_far)

    def y_copy(k):
        return remote(4, k, y_s.at[k, c], y_s.at[k, c], near)

    def loss_step(k, sums):
        asum, bsum, both = sums
        far_copy(1, k, g_chip, g_far).wait_recv()
        far_copy(3, k, b_chip, b_far).wait_recv()
        t = (g_chip[k].astype(F32) + g_far[k].astype(F32)).astype(BF16).astype(F32)
        t_s[k] = t
        branch = b_chip[k].astype(F32) + b_far[k].astype(F32)
        out = (xq[c, :, :, cols(k)] + branch).astype(BF16)
        y_s[k, c] = out
        y_copy(k).start()
        out = out.astype(F32)
        return (
            asum + jnp.sum(out * out, axis=-1, keepdims=True),
            bsum + jnp.sum(t * t, axis=-1, keepdims=True),
            both + jnp.sum(out * t, axis=-1, keepdims=True),
        )

    zero = jnp.zeros((2, quarter, 1), F32)
    asum, bsum, both_sum = lax.fori_loop(0, chunks, loss_step, (zero, zero, zero))
    asum = asum + epsilon
    bsum = bsum + epsilon
    both = lax.rsqrt(asum * bsum)
    cosv = both_sum * both
    slot = (
        lax.broadcasted_iota(jnp.int32, (2, quarter, 1), 0) * (2 * quarter)
        + lax.broadcasted_iota(jnp.int32, (2, quarter, 1), 1)
        + c * quarter
    )
    live = jnp.where(slot < count_ref[0], -math.sqrt(width), 0.0)
    t_factor = live * both
    y_factor = live * cosv / asum

    def dy_copy(k):
        return remote(5, k, dy_s.at[k, c], dy_s.at[k, c], near)

    def dy_step(k, _):
        dy = t_s[k] * t_factor - y_s[k, c].astype(F32) * y_factor
        dy_s[k, c] = dy.astype(BF16)
        dy_copy(k).start()
        dy_own[:, :, cols(k)] = dy
        return 0

    lax.fori_loop(0, chunks, dy_step, 0)

    d_attn_s[...] = jnp.zeros_like(d_attn_s)

    def d_attn_step(k, _):
        dy_copy(k).wait_recv()
        dy = jnp.concatenate(
            [dy_s[k, q % 2, q // 2].astype(F32) for q in range(4)], axis=0
        ).astype(BF16)
        d_attn_s[...] += dot(dy, wo[:, cols(k)], NT)
        return 0

    lax.fori_loop(0, chunks, d_attn_step, 0)

    d_values = jnp.zeros((rows, HD), F32)
    d_keys = jnp.zeros((rows, HD), F32)
    for e in range(QPK):
        probs = probs_s[e]
        d_out = d_attn_s[:, e * HD : (e + 1) * HD].astype(BF16)
        d_values += dot(probs.astype(BF16), d_out, TN)
        dprob = dot(d_out, values, NT)
        dscore = probs * (dprob - jnp.sum(dprob * probs, axis=-1, keepdims=True)) * scale
        dscore_b = dscore.astype(BF16)
        dd_s[:, e * HD : (e + 1) * HD] = dot(dscore_b, keys).astype(BF16)
        d_keys += dot(dscore_b, qkv[:, e * HD : (e + 1) * HD], TN)
    dd_s[:, QPK * HD : (QPK + 1) * HD] = d_keys.astype(BF16)
    dd_s[:, (QPK + 1) * HD :] = d_values.astype(BF16)

    def n_pass_on(k):
        near_copy(6, k, n_part, n_near).wait_recv()
        both_parts = n_part[k, c, 1 - y].astype(F32) + n_near[k, 1 - y].astype(F32)
        n_chip[k] = both_parts.astype(BF16)
        far_copy(7, k, n_chip, n_far).start()

    def n_step(k, _):
        val = dot(dd_s[:, 0 : QPK * HD], wq[cols(k), :], NT) + dot(
            dd_s[:, QPK * HD :], wkv[cols(k), :], NT
        )
        split_store(n_part, k, val)
        near_copy(6, k, n_part, n_near).start()

        @pl.when(k > 0)
        def _():
            n_pass_on(k - 1)

        return 0

    lax.fori_loop(0, chunks, n_step, 0)
    n_pass_on(chunks - 1)

    def out_step(k, _):
        y_copy(k).wait_recv()
        for q in range(4):
            out_ref[q, :, cols(k)] = y_s[k, q % 2, q // 2]
        return 0

    lax.fori_loop(0, chunks, out_step, 0)

    def sum_step(k, acc):
        far_copy(7, k, n_chip, n_far).wait_recv()
        val = n_part[k, c, y].astype(F32) + n_near[k, y].astype(F32) + n_far[k].astype(F32)
        upper = val * gain_ref[:, cols(k)]
        dn_s[:, cols(k)] = upper
        return acc + jnp.sum(upper * xq[c, y, :, cols(k)], axis=-1, keepdims=True)

    acc = lax.fori_loop(0, chunks, sum_step, jnp.zeros((quarter, 1), F32))
    inv_own = inv_s[y * 2 + c]
    x_factor = inv_own * inv_own * inv_own * (acc / width)

    def grad_step(k, _):
        dx = inv_own * dn_s[:, cols(k)] - xq[c, y, :, cols(k)] * x_factor
        grad_ref[:, cols(k)] = (dy_own[y, :, cols(k)] + dx).astype(BF16)
        return 0

    lax.fori_loop(0, chunks, grad_step, 0)

    def drain(k, _):
        near_copy(0, k, g_part, g_near).wait_send()
        far_copy(1, k, g_chip, g_far).wait_send()
        near_copy(2, k, b_part, b_near).wait_send()
        far_copy(3, k, b_chip, b_far).wait_send()
        y_copy(k).wait_send()
        dy_copy(k).wait_send()
        near_copy(6, k, n_part, n_near).wait_send()
        far_copy(7, k, n_chip, n_far).wait_send()
        return 0

    lax.fori_loop(0, chunks, drain, 0)

    @pl.when(s < n_seq - 1)
    def _():
        shift_copy(s + 1).wait_send()


def chunk_of(width):
    for size in (512, 256, 128):
        if width % size == 0:
            return size
    return width


def fused_body(
    teacher_hidden,
    proj_weight,
    student_in,
    norm_gain,
    w_query,
    w_keyval,
    w_out,
    row_offsets,
    row_counts,
    doc_start,
):
    rows, width = student_in.shape
    depth = teacher_hidden.shape[1]
    heads = w_query.shape[1]
    quarter = rows // 4
    chunk = chunk_of(width)
    k = width // chunk
    vmem = pltpu.VMEM
    half = (k, 2, quarter, chunk)
    parts = (k, 2, 2, quarter, chunk)
    scratch = [
        vmem((rows, depth), BF16),
        vmem((k, depth, chunk), BF16),
        vmem((rows, width), BF16),
        vmem(w_query.shape, BF16),
        vmem(w_keyval.shape, BF16),
        vmem(w_out.shape, BF16),
        vmem((2, 2, quarter, width), F32),
        vmem((rows, width), BF16),
        vmem((4, quarter, 1), F32),
        vmem((rows, 2 * heads), BF16),
        vmem((QPK, rows, rows), F32),
        vmem((rows, heads), BF16),
        vmem(parts, BF16),
        vmem(half, BF16),
        vmem(half, BF16),
        vmem(half, BF16),
        vmem(parts, BF16),
        vmem(half, BF16),
        vmem(half, BF16),
        vmem(half, BF16),
        vmem(half, F32),
        vmem(parts, BF16),
        vmem(parts, BF16),
        vmem((2, quarter, width), F32),
        vmem((rows, heads), F32),
        vmem((rows, 2 * heads), BF16),
        vmem(parts, BF16),
        vmem(half, BF16),
        vmem((k, quarter, chunk), BF16),
        vmem((k, quarter, chunk), BF16),
        vmem((quarter, width), F32),
        pltpu.SemaphoreType.DMA((5,)),
        pltpu.SemaphoreType.DMA((k,)),
        pltpu.SemaphoreType.DMA((8, k)),
        pltpu.SemaphoreType.DMA((8, k)),
        pltpu.SemaphoreType.DMA((2,)),
    ]
    smem = pl.BlockSpec(memory_space=pltpu.SMEM)
    in_vmem = pl.BlockSpec(memory_space=pltpu.VMEM)
    anywhere = pl.BlockSpec(memory_space=pl.ANY)
    flops = 2 * rows * width * (depth + 6 * heads)
    moved = 2 * width * (depth + 3 * heads + 3 * rows)
    student_out, grad_in = pl.pallas_call(
        functools.partial(step_kernel, lax.axis_size("seq")),
        out_shape=(
            jax.ShapeDtypeStruct((4, quarter, width), BF16),
            jax.ShapeDtypeStruct((quarter, width), BF16),
        ),
        in_specs=[smem, smem, in_vmem, in_vmem] + [anywhere] * 6,
        out_specs=(in_vmem, in_vmem),
        scratch_shapes=scratch,
        cost_estimate=pl.CostEstimate(flops=flops, bytes_accessed=moved, transcendentals=0),
        compiler_params=pltpu.CompilerParams(
            collective_id=0, has_side_effects=True, vmem_limit_bytes=VMEM_BYTES
        ),
    )(
        row_offsets,
        row_counts,
        doc_start.reshape(1, rows),
        norm_gain.reshape(1, width),
        teacher_hidden,
        proj_weight,
        student_in,
        w_query,
        w_keyval,
        w_out,
    )
    return (student_out.reshape(rows, width), grad_in)


VMEM_BYTES = 52 * 2**20


def solution(mesh):
    in_specs = (
        P("seq", "tp"),
        P("tp", None),
        P("seq", None),
        P(),
        P(None, "tp"),
        P(None, "tp"),
        P("tp", None),
        P("seq"),
        P("seq"),
        P("seq"),
    )
    out_specs = (P("seq", None), P(("seq", "tp"), None))
    body = fused_body if mesh.shape["tp"] == 4 else plain_body
    return jax.shard_map(body, mesh=mesh, in_specs=in_specs, out_specs=out_specs, check_vma=False)
```

```python
import functools
import math

import jax
import jax.numpy as jnp
from jax import lax
from jax.experimental import pallas as pl
from jax.experimental.pallas import tpu as pltpu
from jax.sharding import PartitionSpec as P

HD = 128
QPK = 2


epsilon = 1e-06


def from_behind(block, axis, distance):
    devices = range(lax.axis_size(axis))
    route = [(i - distance, i) for i in devices if i - distance in devices]
    return lax.ppermute(block, axis, route)


def plain_body(
    teacher_hidden,
    proj_weight,
    student_in,
    norm_gain,
    w_query,
    w_keyval,
    w_out,
    row_offsets,
    row_counts,
    doc_start,
):
    scale = 1.0 / math.sqrt(HD)
    tokens_here = teacher_hidden.shape[0]
    quarter = tokens_here // 4
    slots_here = student_in.shape[0]
    width = student_in.shape[1]
    start = row_offsets[0] - lax.axis_index("seq") * tokens_here + quarter
    count = row_counts[0]
    xf = student_in.astype(jnp.float32)
    inv = lax.rsqrt(jnp.mean(xf * xf, axis=1, keepdims=True) + epsilon)
    normed = (xf * inv * norm_gain).astype(jnp.bfloat16)
    query = (
        jnp.dot(normed, w_query, preferred_element_type=jnp.float32)
        .astype(jnp.bfloat16)
        .reshape(slots_here, QPK, HD)
    )
    keyval = (
        jnp.dot(normed, w_keyval, preferred_element_type=jnp.float32)
        .astype(jnp.bfloat16)
        .reshape(slots_here, 2, HD)
    )
    keys = keyval[:, 0, :]
    values = keyval[:, 1, :]
    slots = jnp.arange(slots_here, dtype=jnp.int32)
    allowed = (slots[None, :] >= doc_start[:, None]) & (slots[None, :] <= slots[:, None])
    scores = jnp.einsum("peh,kh->epk", query, keys, preferred_element_type=jnp.float32) * scale
    scores = jnp.where(allowed[None], scores, -jnp.inf)
    top = jnp.max(scores, axis=-1, keepdims=True)
    expo = jnp.exp(scores - top)
    probs = expo / jnp.sum(expo, axis=-1, keepdims=True)
    probs_b = probs.astype(jnp.bfloat16)
    attn = jnp.einsum("epk,kh->peh", probs_b, values, preferred_element_type=jnp.float32).astype(
        jnp.bfloat16
    )
    attn = attn.reshape(slots_here, QPK * HD)
    branch_part = jnp.dot(attn, w_out, preferred_element_type=jnp.float32).astype(jnp.bfloat16)
    earlier = from_behind(teacher_hidden[tokens_here - quarter :], "seq", 1)
    features = jnp.concatenate(
        [earlier, teacher_hidden, jnp.zeros((quarter, teacher_hidden.shape[1]), jnp.bfloat16)],
        axis=0,
    )
    picked = lax.dynamic_slice_in_dim(features, start, slots_here, 0)
    projected = jnp.dot(picked, proj_weight, preferred_element_type=jnp.float32).astype(
        jnp.bfloat16
    )
    goal_sum, branch = (
        lax.psum(projected, "tp").astype(jnp.float32),
        lax.psum(branch_part, "tp").astype(jnp.float32),
    )
    goal = goal_sum.astype(jnp.bfloat16)
    student_out = (xf + branch).astype(jnp.bfloat16)
    yf = student_out.astype(jnp.float32)
    tf = goal.astype(jnp.float32)
    live = (slots < count).astype(jnp.float32)[:, None]
    asum = jnp.sum(yf * yf, axis=1, keepdims=True) + epsilon
    bsum = jnp.sum(tf * tf, axis=1, keepdims=True) + epsilon
    both = lax.rsqrt(asum * bsum)
    cosv = jnp.sum(yf * tf, axis=1, keepdims=True) * both
    dy = -math.sqrt(width) * live * (tf * both - cosv * yf / asum)
    dy_b = dy.astype(jnp.bfloat16)
    d_attn = lax.dot_general(
        dy_b, w_out, (((1,), (1,)), ((), ())), preferred_element_type=jnp.float32
    ).astype(jnp.bfloat16)
    d_out = d_attn.reshape(slots_here, QPK, HD)
    d_values = jnp.einsum("epk,peh->kh", probs_b, d_out, preferred_element_type=jnp.float32).astype(
        jnp.bfloat16
    )
    dprob = jnp.einsum("peh,kh->epk", d_out, values, preferred_element_type=jnp.float32)
    dscore = probs * (dprob - jnp.sum(dprob * probs, axis=-1, keepdims=True)) * scale
    dscore_b = dscore.astype(jnp.bfloat16)
    d_query = jnp.einsum("epk,kh->peh", dscore_b, keys, preferred_element_type=jnp.float32).astype(
        jnp.bfloat16
    )
    d_query = d_query.reshape(slots_here, QPK * HD)
    d_keys = jnp.einsum("epk,peh->kh", dscore_b, query, preferred_element_type=jnp.float32).astype(
        jnp.bfloat16
    )
    d_keyval = jnp.stack([d_keys, d_values], axis=1).reshape(slots_here, 2 * HD)
    own_rows = slots_here // lax.axis_size("tp")
    total = lax.dot_general(
        d_query, w_query, (((1,), (1,)), ((), ())), preferred_element_type=jnp.float32
    )
    d_normed = lax.psum_scatter(
        (
            total
            + lax.dot_general(
                d_keyval, w_keyval, (((1,), (1,)), ((), ())), preferred_element_type=jnp.float32
            )
        ).astype(jnp.bfloat16),
        "tp",
        scatter_dimension=0,
        tiled=True,
    ).astype(jnp.float32)
    first_row = lax.axis_index("tp") * own_rows
    x_own = lax.dynamic_slice_in_dim(xf, first_row, own_rows, 0)
    inv_own = lax.dynamic_slice_in_dim(inv, first_row, own_rows, 0)
    dy_own = lax.dynamic_slice_in_dim(dy, first_row, own_rows, 0)
    upper = d_normed * norm_gain
    dx = inv_own * upper - x_own * inv_own * inv_own * inv_own * jnp.mean(
        upper * x_own, axis=1, keepdims=True
    )
    grad_in = (dy_own + dx).astype(jnp.bfloat16)
    return (student_out, grad_in)


MESH = pl.DeviceIdType.MESH
NT = (((1,), (1,)), ((), ()))
TN = (((0,), (0,)), ((), ()))
F32 = jnp.float32
BF16 = jnp.bfloat16


def dot(a, b, dims=None):
    if dims is None:
        return jnp.dot(a, b, preferred_element_type=F32)
    return lax.dot_general(a, b, dims, preferred_element_type=F32)


def step_kernel(
    n_seq,
    offset_ref,
    count_ref,
    start_hbm,
    gain_hbm,
    teacher_hbm,
    proj_hbm,
    x_hbm,
    wq_hbm,
    wkv_hbm,
    wo_hbm,
    out_ref,
    grad_ref,
    start_s,
    gain_s,
    feat,
    proj,
    x_in,
    wq,
    wkv,
    wo,
    xq,
    normed,
    inv_s,
    qkv,
    probs_s,
    attn_s,
    g_part,
    g_near,
    g_chip,
    g_far,
    b_part,
    b_near,
    b_chip,
    b_far,
    t_s,
    y_s,
    dy_s,
    dy_own,
    d_attn_s,
    dd_s,
    n_part,
    n_near,
    n_chip,
    n_far,
    dn_s,
    load_sem,
    proj_sem,
    send_sem,
    recv_sem,
    shift_sem,
    out_sem,
):
    rows, width = x_in.shape
    quarter = rows // 4
    chunks, _, chunk = proj.shape
    own_tokens = teacher_hbm.shape[0]
    shift = rows - own_tokens
    s = lax.axis_index("seq")
    me = lax.axis_index("tp")
    c = lax.rem(me, 2)
    y = me // 2
    near = {"tp": y * 2 + 1 - c}
    far = {"tp": (1 - y) * 2 + c}
    scale = 1.0 / math.sqrt(HD)

    def gain(k):
        return gain_s[cols(k)][None, :]

    def cols(k):
        return pl.ds(pl.multiple_of(k * chunk, chunk), chunk)

    loads = [
        pltpu.make_async_copy(a, b, load_sem.at[i])
        for i, (a, b) in enumerate(
            [
                (x_hbm, x_in),
                (wq_hbm, wq),
                (wkv_hbm, wkv),
                (teacher_hbm, feat.at[pl.ds(shift, own_tokens)]),
                (wo_hbm, wo),
                (start_hbm, start_s),
                (gain_hbm, gain_s),
            ]
        )
    ]
    loads[3].start()
    loads[0].start()

    def proj_load(k):
        return pltpu.make_async_copy(proj_hbm.at[:, cols(k)], proj.at[k], proj_sem.at[k])

    def start_proj(k, _):
        proj_load(k).start()
        return 0

    lax.fori_loop(0, chunks, start_proj, 0)
    for i in (1, 2, 6, 5, 4):
        loads[i].start()

    barrier = pltpu.get_barrier_semaphore()
    pl.semaphore_signal(barrier, inc=1, device_id=near, device_id_type=MESH)
    pl.semaphore_signal(barrier, inc=1, device_id=far, device_id_type=MESH)

    @pl.when(s > 0)
    def _():
        pl.semaphore_signal(barrier, inc=1, device_id={"seq": s - 1}, device_id_type=MESH)

    @pl.when(s < n_seq - 1)
    def _():
        pl.semaphore_signal(barrier, inc=1, device_id={"seq": s + 1}, device_id_type=MESH)

    inner = (s > 0) & (s < n_seq - 1)

    @pl.when(inner)
    def _():
        pl.semaphore_wait(barrier, 4)

    @pl.when(jnp.logical_not(inner))
    def _():
        pl.semaphore_wait(barrier, 3)

    def shift_copy(to):
        return pltpu.make_async_remote_copy(
            src_ref=teacher_hbm.at[pl.ds(own_tokens - shift, shift)],
            dst_ref=feat.at[pl.ds(0, shift)],
            send_sem=shift_sem.at[0],
            recv_sem=shift_sem.at[1],
            device_id={"seq": to},
            device_id_type=MESH,
        )

    @pl.when(s < n_seq - 1)
    def _():
        shift_copy(s + 1).start()

    @pl.when(s == 0)
    def _():
        feat[0:shift, :] = jnp.zeros((shift, feat.shape[1]), BF16)

    def remote(kind, k, src, dst, to):
        return pltpu.make_async_remote_copy(
            src_ref=src,
            dst_ref=dst,
            send_sem=send_sem.at[kind, k],
            recv_sem=recv_sem.at[kind, k],
            device_id=to,
            device_id_type=MESH,
        )

    def split_store(ref, k, val):
        for q in range(4):
            ref[k, q % 2, q // 2] = val[q * quarter : (q + 1) * quarter].astype(BF16)

    loads[0].wait()

    def square(k, acc):
        v = x_in[:, cols(k)].astype(F32)
        for q in range(4):
            xq[q % 2, q // 2, :, cols(k)] = v[q * quarter : (q + 1) * quarter]
        return acc + jnp.sum(v * v, axis=1, keepdims=True)

    total = lax.fori_loop(0, chunks, square, jnp.zeros((rows, 1), F32))
    inv = lax.rsqrt(total / width + epsilon)
    for q in range(4):
        inv_s[q] = inv[q * quarter : (q + 1) * quarter]

    start = offset_ref[0] - s * own_tokens + shift
    r_i = lax.broadcasted_iota(jnp.int32, (rows, rows), 0)
    c_i = lax.broadcasted_iota(jnp.int32, (rows, rows), 1)

    @pl.when(s > 0)
    def _():
        shift_copy(s).wait_recv()

    loads[3].wait()
    select = jnp.where(c_i == r_i + start, 1.0, 0.0).astype(BF16)
    feat[...] = dot(select, feat[...]).astype(BF16)

    def near_copy(kind, k, part, land):
        return remote(kind, k, part.at[k, 1 - c], land.at[k], near)

    def far_copy(kind, k, chip, land):
        return remote(kind, k, chip.at[k], land.at[k], far)

    def pass_on(kind, k, part, land, chip, far_land):
        near_copy(kind, k, part, land).wait_recv()
        pair = part[k, c, 1 - y].astype(F32) + land[k, 1 - y].astype(F32)
        chip[k] = pair.astype(BF16)
        far_copy(kind + 1, k, chip, far_land).start()

    def own_sum(kind, k, part, land, chip, far_land):
        far_copy(kind + 1, k, chip, far_land).wait_recv()
        return (
            part[k, c, y].astype(F32) + land[k, y].astype(F32) + far_land[k].astype(F32)
        )

    lag = min(2, chunks)

    def scatter(kind, make, part, land, chip, far_land):
        def step(k, _):
            split_store(part, k, make(k))
            near_copy(kind, k, part, land).start()

            @pl.when(k >= lag)
            def _():
                pass_on(kind, k - lag, part, land, chip, far_land)

            return 0

        lax.fori_loop(0, chunks, step, 0)

    def scatter_rest(kind, part, land, chip, far_land):
        for k in range(chunks - lag, chunks):
            pass_on(kind, k, part, land, chip, far_land)

    def project(k):
        proj_load(k).wait()
        return dot(feat[...], proj[k])

    goal_bufs = (g_part, g_near, g_chip, g_far)
    scatter(0, project, *goal_bufs)
    loads[6].wait()

    def norm(k, _):
        v = x_in[:, cols(k)].astype(F32)
        normed[:, cols(k)] = (v * inv * gain(k)).astype(BF16)
        return 0

    lax.fori_loop(0, chunks, norm, 0)

    loads[1].wait()
    loads[2].wait()
    qkv[:, 0 : QPK * HD] = dot(normed[...], wq[...]).astype(BF16)
    scatter_rest(0, *goal_bufs)
    qkv[:, QPK * HD :] = dot(normed[...], wkv[...]).astype(BF16)
    loads[5].wait()

    starts = jnp.sum(
        jnp.where(r_i == c_i, start_s[...][None, :].astype(F32), 0.0), axis=1, keepdims=True
    )
    c_f = c_i.astype(F32)
    allowed = (c_f >= starts) & (c_i <= r_i)
    keys = qkv[:, QPK * HD : (QPK + 1) * HD]
    values = qkv[:, (QPK + 1) * HD :]
    for e in range(QPK):
        scores = dot(qkv[:, e * HD : (e + 1) * HD], keys, NT) * scale
        scores = jnp.where(allowed, scores, -jnp.inf)
        expo = jnp.exp(scores - jnp.max(scores, axis=-1, keepdims=True))
        probs = expo / jnp.sum(expo, axis=-1, keepdims=True)
        probs_s[e] = probs
        attn_s[:, e * HD : (e + 1) * HD] = dot(probs.astype(BF16), values).astype(BF16)

    loads[4].wait()

    branch_bufs = (b_part, b_near, b_chip, b_far)
    scatter(2, lambda k: dot(attn_s[...], wo[:, cols(k)]), *branch_bufs)
    scatter_rest(2, *branch_bufs)

    def y_copy(kind, k, owner, to):
        return remote(kind, k, y_s.at[k, c, owner], y_s.at[k, c, owner], to)

    def dy_copy(kind, k, owner, to):
        return remote(kind, k, dy_s.at[k, c, owner], dy_s.at[k, c, owner], to)

    def loss_step(k, sums):
        asum, bsum, both = sums
        t = own_sum(0, k, *goal_bufs).astype(BF16).astype(F32)
        t_s[k] = t
        out = (xq[c, y, :, cols(k)] + own_sum(2, k, *branch_bufs)).astype(BF16)
        y_s[k, c, y] = out
        y_copy(5, k, y, near).start()
        out = out.astype(F32)
        return (
            asum + jnp.sum(out * out, axis=-1, keepdims=True),
            bsum + jnp.sum(t * t, axis=-1, keepdims=True),
            both + jnp.sum(out * t, axis=-1, keepdims=True),
        )

    zero = jnp.zeros((quarter, 1), F32)
    asum, bsum, both_sum = lax.fori_loop(0, chunks, loss_step, (zero, zero, zero))
    early = min(2, chunks)

    def start_y(k, _):
        y_copy(4, k, y, far).start()
        return 0

    lax.fori_loop(0, early, start_y, 0)
    asum = asum + epsilon
    bsum = bsum + epsilon
    both = lax.rsqrt(asum * bsum)
    cosv = both_sum * both
    slot = lax.broadcasted_iota(jnp.int32, (quarter, 1), 0) + (2 * y + c) * quarter
    live = jnp.where(slot < count_ref[0], -math.sqrt(width), 0.0)
    t_factor = live * both
    y_factor = live * cosv / asum

    def dy_step(k, _):
        dy = t_s[k] * t_factor - y_s[k, c, y].astype(F32) * y_factor
        dy_s[k, c, y] = dy.astype(BF16)
        dy_copy(7, k, y, far).start()
        dy_copy(8, k, y, near).start()
        dy_own[:, cols(k)] = dy
        return 0

    lax.fori_loop(0, chunks, dy_step, 0)

    d_attn_s[...] = jnp.zeros_like(d_attn_s)

    def d_attn_part(k):
        dy_copy(8, k, y, near).wait_recv()
        dy_copy(9, k, 1 - y, near).wait_recv()
        dy = jnp.concatenate(
            [dy_s[k, q % 2, q // 2].astype(F32) for q in range(4)], axis=0
        ).astype(BF16)
        d_attn_s[...] += dot(dy, wo[:, cols(k)], NT)

    def d_attn_step(k, _):
        dy_copy(7, k, y, far).wait_recv()
        dy_copy(9, k, 1 - y, near).start()

        @pl.when(k > 0)
        def _():
            d_attn_part(k - 1)

        return 0

    lax.fori_loop(0, chunks, d_attn_step, 0)
    lax.fori_loop(early, chunks, start_y, 0)
    d_attn_part(chunks - 1)

    d_values = jnp.zeros((rows, HD), F32)
    d_keys = jnp.zeros((rows, HD), F32)
    for e in range(QPK):
        probs = probs_s[e]
        d_out = d_attn_s[:, e * HD : (e + 1) * HD].astype(BF16)
        d_values += dot(probs.astype(BF16), d_out, TN)
        dprob = dot(d_out, values, NT)
        dscore = probs * (dprob - jnp.sum(dprob * probs, axis=-1, keepdims=True)) * scale
        dscore_b = dscore.astype(BF16)
        dd_s[:, e * HD : (e + 1) * HD] = dot(dscore_b, keys).astype(BF16)
        d_keys += dot(dscore_b, qkv[:, e * HD : (e + 1) * HD], TN)
    dd_s[:, QPK * HD : (QPK + 1) * HD] = d_keys.astype(BF16)
    dd_s[:, (QPK + 1) * HD :] = d_values.astype(BF16)

    def d_normed(k):
        return dot(dd_s[:, 0 : QPK * HD], wq[cols(k), :], NT) + dot(
            dd_s[:, QPK * HD :], wkv[cols(k), :], NT
        )

    n_bufs = (n_part, n_near, n_chip, n_far)
    scatter(10, d_normed, *n_bufs)
    scatter_rest(10, *n_bufs)

    def forward_y(k, _):
        y_copy(4, k, y, far).wait_recv()
        y_copy(6, k, 1 - y, near).start()
        return 0

    lax.fori_loop(0, chunks, forward_y, 0)

    def out_copy(k, q):
        return pltpu.make_async_copy(
            y_s.at[k, q % 2, q // 2], out_ref.at[q, :, cols(k)], out_sem.at[k, q]
        )

    def out_step(k, _):
        y_copy(5, k, y, near).wait_recv()
        y_copy(6, k, 1 - y, near).wait_recv()
        for q in range(4):
            out_copy(k, q).start()
        return 0

    lax.fori_loop(0, chunks, out_step, 0)

    def sum_step(k, acc):
        upper = own_sum(10, k, *n_bufs) * gain(k)
        dn_s[:, cols(k)] = upper
        return acc + jnp.sum(upper * xq[c, y, :, cols(k)], axis=-1, keepdims=True)

    acc = lax.fori_loop(0, chunks, sum_step, zero)
    inv_own = inv_s[y * 2 + c]
    x_factor = inv_own * inv_own * inv_own * (acc / width)

    def grad_step(k, _):
        dx = inv_own * dn_s[:, cols(k)] - xq[c, y, :, cols(k)] * x_factor
        grad_ref[:, cols(k)] = (dy_own[:, cols(k)] + dx).astype(BF16)
        return 0

    lax.fori_loop(0, chunks, grad_step, 0)

    def drain(k, _):
        for q in range(4):
            out_copy(k, q).wait()
        for kind, bufs in ((0, goal_bufs), (2, branch_bufs), (10, n_bufs)):
            near_copy(kind, k, bufs[0], bufs[1]).wait_send()
            far_copy(kind + 1, k, bufs[2], bufs[3]).wait_send()
        for first, copy in ((4, y_copy), (7, dy_copy)):
            copy(first, k, y, far).wait_send()
            copy(first + 1, k, y, near).wait_send()
            copy(first + 2, k, 1 - y, near).wait_send()
        return 0

    lax.fori_loop(0, chunks, drain, 0)

    @pl.when(s < n_seq - 1)
    def _():
        shift_copy(s + 1).wait_send()


def chunk_of(width):
    for size in (512, 256, 128):
        if width % size == 0:
            return size
    return width


def fused_body(
    teacher_hidden,
    proj_weight,
    student_in,
    norm_gain,
    w_query,
    w_keyval,
    w_out,
    row_offsets,
    row_counts,
    doc_start,
):
    rows, width = student_in.shape
    depth = teacher_hidden.shape[1]
    heads = w_query.shape[1]
    quarter = rows // 4
    chunk = chunk_of(width)
    k = width // chunk
    vmem = pltpu.VMEM
    half = (k, 2, quarter, chunk)
    parts = (k, 2, 2, quarter, chunk)
    own = (k, quarter, chunk)
    scratch = [
        vmem((rows,), jnp.int32),
        vmem((width,), F32),
        vmem((rows, depth), BF16),
        vmem((k, depth, chunk), BF16),
        vmem((rows, width), BF16),
        vmem(w_query.shape, BF16),
        vmem(w_keyval.shape, BF16),
        vmem(w_out.shape, BF16),
        vmem((2, 2, quarter, width), F32),
        vmem((rows, width), BF16),
        vmem((4, quarter, 1), F32),
        vmem((rows, 2 * heads), BF16),
        vmem((QPK, rows, rows), F32),
        vmem((rows, heads), BF16),
        vmem(parts, BF16),
        vmem(half, BF16),
        vmem(own, BF16),
        vmem(own, BF16),
        vmem(parts, BF16),
        vmem(half, BF16),
        vmem(own, BF16),
        vmem(own, BF16),
        vmem(own, F32),
        vmem(parts, BF16),
        vmem(parts, BF16),
        vmem((quarter, width), F32),
        vmem((rows, heads), F32),
        vmem((rows, 2 * heads), BF16),
        vmem(parts, BF16),
        vmem(half, BF16),
        vmem(own, BF16),
        vmem(own, BF16),
        vmem((quarter, width), F32),
        pltpu.SemaphoreType.DMA((7,)),
        pltpu.SemaphoreType.DMA((k,)),
        pltpu.SemaphoreType.DMA((12, k)),
        pltpu.SemaphoreType.DMA((12, k)),
        pltpu.SemaphoreType.DMA((2,)),
        pltpu.SemaphoreType.DMA((k, 4)),
    ]
    smem = pl.BlockSpec(memory_space=pltpu.SMEM)
    in_vmem = pl.BlockSpec(memory_space=pltpu.VMEM)
    in_hbm = pl.BlockSpec(memory_space=pltpu.HBM)
    flops = 2 * rows * width * (depth + 6 * heads)
    moved = 2 * width * (depth + 3 * heads + 3 * rows)
    student_out, grad_in = pl.pallas_call(
        functools.partial(step_kernel, lax.axis_size("seq")),
        out_shape=(
            jax.ShapeDtypeStruct((4, quarter, width), BF16),
            jax.ShapeDtypeStruct((quarter, width), BF16),
        ),
        in_specs=[smem, smem] + [in_hbm] * 8,
        out_specs=(in_hbm, in_vmem),
        scratch_shapes=scratch,
        cost_estimate=pl.CostEstimate(flops=flops, bytes_accessed=moved, transcendentals=0),
        compiler_params=pltpu.CompilerParams(
            collective_id=0, has_side_effects=True, vmem_limit_bytes=VMEM_BYTES
        ),
    )(
        row_offsets,
        row_counts,
        doc_start,
        norm_gain,
        teacher_hidden,
        proj_weight,
        student_in,
        w_query,
        w_keyval,
        w_out,
    )
    return (student_out.reshape(rows, width), grad_in)


VMEM_BYTES = 60 * 2**20


def solution(mesh):
    in_specs = (
        P("seq", "tp"),
        P("tp", None),
        P("seq", None),
        P(),
        P(None, "tp"),
        P(None, "tp"),
        P("tp", None),
        P("seq"),
        P("seq"),
        P("seq"),
    )
    out_specs = (P("seq", None), P(("seq", "tp"), None))
    body = fused_body if mesh.shape["tp"] == 4 else plain_body
    return jax.shard_map(body, mesh=mesh, in_specs=in_specs, out_specs=out_specs, check_vma=False)
```

```python
import functools
import math

import jax
import jax.numpy as jnp
from jax import lax
from jax.experimental import pallas as pl
from jax.experimental.pallas import tpu as pltpu
from jax.sharding import PartitionSpec as P

HD = 128
QPK = 2


epsilon = 1e-06


def from_behind(block, axis, distance):
    devices = range(lax.axis_size(axis))
    route = [(i - distance, i) for i in devices if i - distance in devices]
    return lax.ppermute(block, axis, route)


def plain_body(
    teacher_hidden,
    proj_weight,
    student_in,
    norm_gain,
    w_query,
    w_keyval,
    w_out,
    row_offsets,
    row_counts,
    doc_start,
):
    scale = 1.0 / math.sqrt(HD)
    tokens_here = teacher_hidden.shape[0]
    quarter = tokens_here // 4
    slots_here = student_in.shape[0]
    width = student_in.shape[1]
    start = row_offsets[0] - lax.axis_index("seq") * tokens_here + quarter
    count = row_counts[0]
    xf = student_in.astype(jnp.float32)
    inv = lax.rsqrt(jnp.mean(xf * xf, axis=1, keepdims=True) + epsilon)
    normed = (xf * inv * norm_gain).astype(jnp.bfloat16)
    query = (
        jnp.dot(normed, w_query, preferred_element_type=jnp.float32)
        .astype(jnp.bfloat16)
        .reshape(slots_here, QPK, HD)
    )
    keyval = (
        jnp.dot(normed, w_keyval, preferred_element_type=jnp.float32)
        .astype(jnp.bfloat16)
        .reshape(slots_here, 2, HD)
    )
    keys = keyval[:, 0, :]
    values = keyval[:, 1, :]
    slots = jnp.arange(slots_here, dtype=jnp.int32)
    allowed = (slots[None, :] >= doc_start[:, None]) & (slots[None, :] <= slots[:, None])
    scores = jnp.einsum("peh,kh->epk", query, keys, preferred_element_type=jnp.float32) * scale
    scores = jnp.where(allowed[None], scores, -jnp.inf)
    top = jnp.max(scores, axis=-1, keepdims=True)
    expo = jnp.exp(scores - top)
    probs = expo / jnp.sum(expo, axis=-1, keepdims=True)
    probs_b = probs.astype(jnp.bfloat16)
    attn = jnp.einsum("epk,kh->peh", probs_b, values, preferred_element_type=jnp.float32).astype(
        jnp.bfloat16
    )
    attn = attn.reshape(slots_here, QPK * HD)
    branch_part = jnp.dot(attn, w_out, preferred_element_type=jnp.float32).astype(jnp.bfloat16)
    earlier = from_behind(teacher_hidden[tokens_here - quarter :], "seq", 1)
    features = jnp.concatenate(
        [earlier, teacher_hidden, jnp.zeros((quarter, teacher_hidden.shape[1]), jnp.bfloat16)],
        axis=0,
    )
    picked = lax.dynamic_slice_in_dim(features, start, slots_here, 0)
    projected = jnp.dot(picked, proj_weight, preferred_element_type=jnp.float32).astype(
        jnp.bfloat16
    )
    goal_sum, branch = (
        lax.psum(projected, "tp").astype(jnp.float32),
        lax.psum(branch_part, "tp").astype(jnp.float32),
    )
    goal = goal_sum.astype(jnp.bfloat16)
    student_out = (xf + branch).astype(jnp.bfloat16)
    yf = student_out.astype(jnp.float32)
    tf = goal.astype(jnp.float32)
    live = (slots < count).astype(jnp.float32)[:, None]
    asum = jnp.sum(yf * yf, axis=1, keepdims=True) + epsilon
    bsum = jnp.sum(tf * tf, axis=1, keepdims=True) + epsilon
    both = lax.rsqrt(asum * bsum)
    cosv = jnp.sum(yf * tf, axis=1, keepdims=True) * both
    dy = -math.sqrt(width) * live * (tf * both - cosv * yf / asum)
    dy_b = dy.astype(jnp.bfloat16)
    d_attn = lax.dot_general(
        dy_b, w_out, (((1,), (1,)), ((), ())), preferred_element_type=jnp.float32
    ).astype(jnp.bfloat16)
    d_out = d_attn.reshape(slots_here, QPK, HD)
    d_values = jnp.einsum("epk,peh->kh", probs_b, d_out, preferred_element_type=jnp.float32).astype(
        jnp.bfloat16
    )
    dprob = jnp.einsum("peh,kh->epk", d_out, values, preferred_element_type=jnp.float32)
    dscore = probs * (dprob - jnp.sum(dprob * probs, axis=-1, keepdims=True)) * scale
    dscore_b = dscore.astype(jnp.bfloat16)
    d_query = jnp.einsum("epk,kh->peh", dscore_b, keys, preferred_element_type=jnp.float32).astype(
        jnp.bfloat16
    )
    d_query = d_query.reshape(slots_here, QPK * HD)
    d_keys = jnp.einsum("epk,peh->kh", dscore_b, query, preferred_element_type=jnp.float32).astype(
        jnp.bfloat16
    )
    d_keyval = jnp.stack([d_keys, d_values], axis=1).reshape(slots_here, 2 * HD)
    own_rows = slots_here // lax.axis_size("tp")
    total = lax.dot_general(
        d_query, w_query, (((1,), (1,)), ((), ())), preferred_element_type=jnp.float32
    )
    d_normed = lax.psum_scatter(
        (
            total
            + lax.dot_general(
                d_keyval, w_keyval, (((1,), (1,)), ((), ())), preferred_element_type=jnp.float32
            )
        ).astype(jnp.bfloat16),
        "tp",
        scatter_dimension=0,
        tiled=True,
    ).astype(jnp.float32)
    first_row = lax.axis_index("tp") * own_rows
    x_own = lax.dynamic_slice_in_dim(xf, first_row, own_rows, 0)
    inv_own = lax.dynamic_slice_in_dim(inv, first_row, own_rows, 0)
    dy_own = lax.dynamic_slice_in_dim(dy, first_row, own_rows, 0)
    upper = d_normed * norm_gain
    dx = inv_own * upper - x_own * inv_own * inv_own * inv_own * jnp.mean(
        upper * x_own, axis=1, keepdims=True
    )
    grad_in = (dy_own + dx).astype(jnp.bfloat16)
    return (student_out, grad_in)


MESH = pl.DeviceIdType.MESH
NT = (((1,), (1,)), ((), ()))
TN = (((0,), (0,)), ((), ()))
F32 = jnp.float32
BF16 = jnp.bfloat16


def dot(a, b, dims=None):
    if dims is None:
        return jnp.dot(a, b, preferred_element_type=F32)
    return lax.dot_general(a, b, dims, preferred_element_type=F32)


def step_kernel(
    n_seq,
    offset_ref,
    count_ref,
    start_hbm,
    gain_hbm,
    teacher_hbm,
    proj_hbm,
    x_hbm,
    wq_hbm,
    wkv_hbm,
    wo_hbm,
    out_ref,
    grad_ref,
    start_s,
    gain_s,
    feat,
    proj,
    x_in,
    wq,
    wkv,
    wo,
    xq,
    normed,
    inv_s,
    qkv,
    probs_s,
    attn_s,
    g_part,
    g_near,
    g_chip,
    g_far,
    b_part,
    b_near,
    b_chip,
    b_far,
    t_s,
    y_s,
    dy_s,
    dy_own,
    d_attn_s,
    dd_s,
    n_part,
    n_near,
    n_chip,
    n_far,
    dn_s,
    load_sem,
    proj_sem,
    send_sem,
    recv_sem,
    shift_sem,
    out_sem,
):
    rows, width = x_in.shape
    quarter = rows // 4
    chunks, _, chunk = proj.shape
    own_tokens = teacher_hbm.shape[0]
    shift = rows - own_tokens
    s = lax.axis_index("seq")
    me = lax.axis_index("tp")
    c = lax.rem(me, 2)
    y = me // 2
    near = {"tp": y * 2 + 1 - c}
    far = {"tp": (1 - y) * 2 + c}
    scale = 1.0 / math.sqrt(HD)

    barrier = pltpu.get_barrier_semaphore()
    pl.semaphore_signal(barrier, inc=1, device_id=near, device_id_type=MESH)
    pl.semaphore_signal(barrier, inc=1, device_id=far, device_id_type=MESH)

    @pl.when(s > 0)
    def _():
        pl.semaphore_signal(barrier, inc=1, device_id={"seq": s - 1}, device_id_type=MESH)

    @pl.when(s < n_seq - 1)
    def _():
        pl.semaphore_signal(barrier, inc=1, device_id={"seq": s + 1}, device_id_type=MESH)

    def gain(k):
        return gain_s[cols(k)][None, :]

    def cols(k):
        return pl.ds(pl.multiple_of(k * chunk, chunk), chunk)

    loads = [
        pltpu.make_async_copy(a, b, load_sem.at[i])
        for i, (a, b) in enumerate(
            [
                (x_hbm, x_in),
                (wq_hbm, wq),
                (wkv_hbm, wkv),
                (teacher_hbm, feat.at[pl.ds(shift, own_tokens)]),
                (wo_hbm, wo),
                (start_hbm, start_s),
                (gain_hbm, gain_s),
            ]
        )
    ]
    for i in (0, 6, 3, 1):
        loads[i].start()

    def proj_load(k):
        return pltpu.make_async_copy(proj_hbm.at[:, cols(k)], proj.at[k], proj_sem.at[k])

    def start_proj(k, _):
        proj_load(k).start()
        return 0

    lax.fori_loop(0, chunks, start_proj, 0)
    for i in (2, 5, 4):
        loads[i].start()

    loads[0].wait()

    def square(k, acc):
        v = x_in[:, cols(k)].astype(F32)
        for q in range(4):
            xq[q % 2, q // 2, :, cols(k)] = v[q * quarter : (q + 1) * quarter]
        return acc + jnp.sum(v * v, axis=1, keepdims=True)

    total = lax.fori_loop(0, chunks, square, jnp.zeros((rows, 1), F32))
    inv = lax.rsqrt(total / width + epsilon)
    for q in range(4):
        inv_s[q] = inv[q * quarter : (q + 1) * quarter]

    inner = (s > 0) & (s < n_seq - 1)

    @pl.when(inner)
    def _():
        pl.semaphore_wait(barrier, 4)

    @pl.when(jnp.logical_not(inner))
    def _():
        pl.semaphore_wait(barrier, 3)

    def shift_copy(to):
        return pltpu.make_async_remote_copy(
            src_ref=teacher_hbm.at[pl.ds(own_tokens - shift, shift)],
            dst_ref=feat.at[pl.ds(0, shift)],
            send_sem=shift_sem.at[0],
            recv_sem=shift_sem.at[1],
            device_id={"seq": to},
            device_id_type=MESH,
        )

    @pl.when(s < n_seq - 1)
    def _():
        shift_copy(s + 1).start()

    @pl.when(s == 0)
    def _():
        feat[0:shift, :] = jnp.zeros((shift, feat.shape[1]), BF16)

    def remote(kind, k, src, dst, to):
        return pltpu.make_async_remote_copy(
            src_ref=src,
            dst_ref=dst,
            send_sem=send_sem.at[kind, k],
            recv_sem=recv_sem.at[kind, k],
            device_id=to,
            device_id_type=MESH,
        )

    def split_store(ref, k, val):
        for q in range(4):
            ref[k, q % 2, q // 2] = val[q * quarter : (q + 1) * quarter].astype(BF16)

    loads[6].wait()

    def norm(k, _):
        v = x_in[:, cols(k)].astype(F32)
        normed[:, cols(k)] = (v * inv * gain(k)).astype(BF16)
        return 0

    lax.fori_loop(0, chunks, norm, 0)

    loads[1].wait()
    qkv[:, 0 : QPK * HD] = dot(normed[...], wq[...]).astype(BF16)

    start = offset_ref[0] - s * own_tokens + shift
    r_i = lax.broadcasted_iota(jnp.int32, (rows, rows), 0)
    c_i = lax.broadcasted_iota(jnp.int32, (rows, rows), 1)

    @pl.when(s > 0)
    def _():
        shift_copy(s).wait_recv()

    loads[3].wait()
    select = jnp.where(c_i == r_i + start, 1.0, 0.0).astype(BF16)
    feat[...] = dot(select, feat[...]).astype(BF16)

    def near_copy(kind, k, part, land):
        return remote(kind, k, part.at[k, 1 - c], land.at[k], near)

    def far_copy(kind, k, chip, land):
        return remote(kind, k, chip.at[k], land.at[k], far)

    def pass_on(kind, k, part, land, chip, far_land):
        near_copy(kind, k, part, land).wait_recv()
        pair = part[k, c, 1 - y].astype(F32) + land[k, 1 - y].astype(F32)
        chip[k] = pair.astype(BF16)
        far_copy(kind + 1, k, chip, far_land).start()

    def own_sum(kind, k, part, land, chip, far_land):
        far_copy(kind + 1, k, chip, far_land).wait_recv()
        return (
            part[k, c, y].astype(F32) + land[k, y].astype(F32) + far_land[k].astype(F32)
        )

    lag = min(2, chunks)

    def scatter(kind, make, part, land, chip, far_land):
        def step(k, _):
            split_store(part, k, make(k))
            near_copy(kind, k, part, land).start()

            @pl.when(k >= lag)
            def _():
                pass_on(kind, k - lag, part, land, chip, far_land)

            return 0

        lax.fori_loop(0, chunks, step, 0)

    def scatter_rest(kind, part, land, chip, far_land):
        for k in range(chunks - lag, chunks):
            pass_on(kind, k, part, land, chip, far_land)

    def project(k):
        proj_load(k).wait()
        return dot(feat[...], proj[k])

    goal_bufs = (g_part, g_near, g_chip, g_far)
    scatter(0, project, *goal_bufs)
    loads[2].wait()
    scatter_rest(0, *goal_bufs)
    qkv[:, QPK * HD :] = dot(normed[...], wkv[...]).astype(BF16)
    loads[5].wait()

    starts = jnp.sum(
        jnp.where(r_i == c_i, start_s[...][None, :].astype(F32), 0.0), axis=1, keepdims=True
    )
    c_f = c_i.astype(F32)
    allowed = (c_f >= starts) & (c_i <= r_i)
    keys = qkv[:, QPK * HD : (QPK + 1) * HD]
    values = qkv[:, (QPK + 1) * HD :]
    for e in range(QPK):
        scores = dot(qkv[:, e * HD : (e + 1) * HD], keys, NT) * scale
        scores = jnp.where(allowed, scores, -jnp.inf)
        expo = jnp.exp(scores - jnp.max(scores, axis=-1, keepdims=True))
        probs = expo / jnp.sum(expo, axis=-1, keepdims=True)
        probs_s[e] = probs
        attn_s[:, e * HD : (e + 1) * HD] = dot(probs.astype(BF16), values).astype(BF16)

    loads[4].wait()

    branch_bufs = (b_part, b_near, b_chip, b_far)
    scatter(2, lambda k: dot(attn_s[...], wo[:, cols(k)]), *branch_bufs)
    scatter_rest(2, *branch_bufs)

    def y_copy(kind, k, owner, to):
        return remote(kind, k, y_s.at[k, c, owner], y_s.at[k, c, owner], to)

    def dy_copy(kind, k, owner, to):
        return remote(kind, k, dy_s.at[k, c, owner], dy_s.at[k, c, owner], to)

    def loss_step(k, sums):
        asum, bsum, both = sums
        t = own_sum(0, k, *goal_bufs).astype(BF16).astype(F32)
        t_s[k] = t
        out = (xq[c, y, :, cols(k)] + own_sum(2, k, *branch_bufs)).astype(BF16)
        y_s[k, c, y] = out
        y_copy(5, k, y, near).start()
        out = out.astype(F32)
        return (
            asum + jnp.sum(out * out, axis=-1, keepdims=True),
            bsum + jnp.sum(t * t, axis=-1, keepdims=True),
            both + jnp.sum(out * t, axis=-1, keepdims=True),
        )

    zero = jnp.zeros((quarter, 1), F32)
    asum, bsum, both_sum = lax.fori_loop(0, chunks, loss_step, (zero, zero, zero))
    early = min(2, chunks)

    def start_y(k, _):
        y_copy(4, k, y, far).start()
        return 0

    lax.fori_loop(0, early, start_y, 0)
    asum = asum + epsilon
    bsum = bsum + epsilon
    both = lax.rsqrt(asum * bsum)
    cosv = both_sum * both
    slot = lax.broadcasted_iota(jnp.int32, (quarter, 1), 0) + (2 * y + c) * quarter
    live = jnp.where(slot < count_ref[0], -math.sqrt(width), 0.0)
    t_factor = live * both
    y_factor = live * cosv / asum

    def dy_step(k, _):
        dy = t_s[k] * t_factor - y_s[k, c, y].astype(F32) * y_factor
        dy_s[k, c, y] = dy.astype(BF16)
        dy_copy(7, k, y, far).start()
        dy_copy(8, k, y, near).start()
        dy_own[:, cols(k)] = dy
        return 0

    lax.fori_loop(0, chunks, dy_step, 0)

    d_attn_s[...] = jnp.zeros_like(d_attn_s)

    def d_attn_part(k):
        dy_copy(8, k, y, near).wait_recv()
        dy_copy(9, k, 1 - y, near).wait_recv()
        dy = jnp.concatenate(
            [dy_s[k, q % 2, q // 2].astype(F32) for q in range(4)], axis=0
        ).astype(BF16)
        d_attn_s[...] += dot(dy, wo[:, cols(k)], NT)

    def d_attn_step(k, _):
        dy_copy(7, k, y, far).wait_recv()
        dy_copy(9, k, 1 - y, near).start()

        @pl.when(k > 0)
        def _():
            d_attn_part(k - 1)

        return 0

    lax.fori_loop(0, chunks, d_attn_step, 0)
    lax.fori_loop(early, chunks, start_y, 0)
    d_attn_part(chunks - 1)

    d_values = jnp.zeros((rows, HD), F32)
    d_keys = jnp.zeros((rows, HD), F32)
    for e in range(QPK):
        probs = probs_s[e]
        d_out = d_attn_s[:, e * HD : (e + 1) * HD].astype(BF16)
        d_values += dot(probs.astype(BF16), d_out, TN)
        dprob = dot(d_out, values, NT)
        dscore = probs * (dprob - jnp.sum(dprob * probs, axis=-1, keepdims=True)) * scale
        dscore_b = dscore.astype(BF16)
        dd_s[:, e * HD : (e + 1) * HD] = dot(dscore_b, keys).astype(BF16)
        d_keys += dot(dscore_b, qkv[:, e * HD : (e + 1) * HD], TN)
    dd_s[:, QPK * HD : (QPK + 1) * HD] = d_keys.astype(BF16)
    dd_s[:, (QPK + 1) * HD :] = d_values.astype(BF16)

    def d_normed(k):
        return dot(dd_s[:, 0 : QPK * HD], wq[cols(k), :], NT) + dot(
            dd_s[:, QPK * HD :], wkv[cols(k), :], NT
        )

    n_bufs = (n_part, n_near, n_chip, n_far)
    scatter(10, d_normed, *n_bufs)
    scatter_rest(10, *n_bufs)

    def forward_y(k, _):
        y_copy(4, k, y, far).wait_recv()
        y_copy(6, k, 1 - y, near).start()
        return 0

    lax.fori_loop(0, chunks, forward_y, 0)

    def out_copy(k, q):
        return pltpu.make_async_copy(
            y_s.at[k, q % 2, q // 2], out_ref.at[q, :, cols(k)], out_sem.at[k, q]
        )

    def out_step(k, _):
        y_copy(5, k, y, near).wait_recv()
        y_copy(6, k, 1 - y, near).wait_recv()
        for q in range(4):
            out_copy(k, q).start()
        return 0

    lax.fori_loop(0, chunks, out_step, 0)

    def drain_early(k, _):
        for kind, bufs in ((0, goal_bufs), (2, branch_bufs)):
            near_copy(kind, k, bufs[0], bufs[1]).wait_send()
            far_copy(kind + 1, k, bufs[2], bufs[3]).wait_send()
        for first, copy in ((4, y_copy), (7, dy_copy)):
            copy(first, k, y, far).wait_send()
            copy(first + 1, k, y, near).wait_send()
            copy(first + 2, k, 1 - y, near).wait_send()
        return 0

    lax.fori_loop(0, chunks, drain_early, 0)

    @pl.when(s < n_seq - 1)
    def _():
        shift_copy(s + 1).wait_send()

    def sum_step(k, acc):
        upper = own_sum(10, k, *n_bufs) * gain(k)
        dn_s[:, cols(k)] = upper
        return acc + jnp.sum(upper * xq[c, y, :, cols(k)], axis=-1, keepdims=True)

    acc = lax.fori_loop(0, chunks, sum_step, zero)
    inv_own = inv_s[y * 2 + c]
    x_factor = inv_own * inv_own * inv_own * (acc / width)

    def grad_step(k, _):
        dx = inv_own * dn_s[:, cols(k)] - xq[c, y, :, cols(k)] * x_factor
        grad_ref[:, cols(k)] = (dy_own[:, cols(k)] + dx).astype(BF16)
        return 0

    lax.fori_loop(0, chunks, grad_step, 0)

    def drain(k, _):
        for q in range(4):
            out_copy(k, q).wait()
        near_copy(10, k, n_part, n_near).wait_send()
        far_copy(11, k, n_chip, n_far).wait_send()
        return 0

    lax.fori_loop(0, chunks, drain, 0)


def hand_over(y_ref, g_ref, out_ref, grad_ref, sem):
    copies = [pltpu.make_async_copy(y_ref.at[q], out_ref.at[q], sem.at[q]) for q in range(4)]
    copies.append(pltpu.make_async_copy(g_ref, grad_ref, sem.at[4]))
    for one in copies:
        one.start()
    for one in copies:
        one.wait()


def chunk_of(width):
    for size in (512, 256, 128):
        if width % size == 0:
            return size
    return width


def fused_body(
    teacher_hidden,
    proj_weight,
    student_in,
    norm_gain,
    w_query,
    w_keyval,
    w_out,
    row_offsets,
    row_counts,
    doc_start,
):
    rows, width = student_in.shape
    depth = teacher_hidden.shape[1]
    heads = w_query.shape[1]
    quarter = rows // 4
    chunk = chunk_of(width)
    k = width // chunk
    vmem = pltpu.VMEM
    half = (k, 2, quarter, chunk)
    parts = (k, 2, 2, quarter, chunk)
    own = (k, quarter, chunk)
    scratch = [
        vmem((rows,), jnp.int32),
        vmem((width,), F32),
        vmem((rows, depth), BF16),
        vmem((k, depth, chunk), BF16),
        vmem((rows, width), BF16),
        vmem(w_query.shape, BF16),
        vmem(w_keyval.shape, BF16),
        vmem(w_out.shape, BF16),
        vmem((2, 2, quarter, width), F32),
        vmem((rows, width), BF16),
        vmem((4, quarter, 1), F32),
        vmem((rows, 2 * heads), BF16),
        vmem((QPK, rows, rows), F32),
        vmem((rows, heads), BF16),
        vmem(parts, BF16),
        vmem(half, BF16),
        vmem(own, BF16),
        vmem(own, BF16),
        vmem(parts, BF16),
        vmem(half, BF16),
        vmem(own, BF16),
        vmem(own, BF16),
        vmem(own, F32),
        vmem(parts, BF16),
        vmem(parts, BF16),
        vmem((quarter, width), F32),
        vmem((rows, heads), F32),
        vmem((rows, 2 * heads), BF16),
        vmem(parts, BF16),
        vmem(half, BF16),
        vmem(own, BF16),
        vmem(own, BF16),
        vmem((quarter, width), F32),
        pltpu.SemaphoreType.DMA((7,)),
        pltpu.SemaphoreType.DMA((k,)),
        pltpu.SemaphoreType.DMA((12, k)),
        pltpu.SemaphoreType.DMA((12, k)),
        pltpu.SemaphoreType.DMA((2,)),
        pltpu.SemaphoreType.DMA((k, 4)),
    ]
    smem = pl.BlockSpec(memory_space=pltpu.SMEM)
    in_vmem = pl.BlockSpec(memory_space=pltpu.VMEM)
    in_hbm = pl.BlockSpec(memory_space=pltpu.HBM)
    flops = 2 * rows * width * (depth + 6 * heads)
    moved = 2 * width * (depth + 3 * heads + 3 * rows)
    student_out, grad_in = pl.pallas_call(
        functools.partial(step_kernel, lax.axis_size("seq")),
        out_shape=(
            jax.ShapeDtypeStruct((4, quarter, width), BF16),
            jax.ShapeDtypeStruct((quarter, width), BF16),
        ),
        in_specs=[smem, smem] + [in_hbm] * 8,
        out_specs=(in_hbm, in_vmem),
        scratch_shapes=scratch,
        cost_estimate=pl.CostEstimate(flops=flops, bytes_accessed=moved, transcendentals=0),
        compiler_params=pltpu.CompilerParams(
            collective_id=0, has_side_effects=True, vmem_limit_bytes=VMEM_BYTES
        ),
    )(
        row_offsets,
        row_counts,
        doc_start,
        norm_gain,
        teacher_hidden,
        proj_weight,
        student_in,
        w_query,
        w_keyval,
        w_out,
    )
    student_out, grad_in = pl.pallas_call(
        hand_over,
        out_shape=(
            jax.ShapeDtypeStruct(student_out.shape, BF16),
            jax.ShapeDtypeStruct(grad_in.shape, BF16),
        ),
        in_specs=[in_hbm, in_hbm],
        out_specs=(in_hbm, in_hbm),
        scratch_shapes=[pltpu.SemaphoreType.DMA((5,))],
        compiler_params=pltpu.CompilerParams(vmem_limit_bytes=VMEM_BYTES),
    )(student_out, grad_in)
    return (student_out.reshape(rows, width), grad_in)


VMEM_BYTES = 60 * 2**20


def solution(mesh):
    in_specs = (
        P("seq", "tp"),
        P("tp", None),
        P("seq", None),
        P(),
        P(None, "tp"),
        P(None, "tp"),
        P("tp", None),
        P("seq"),
        P("seq"),
        P("seq"),
    )
    out_specs = (P("seq", None), P(("seq", "tp"), None))
    body = fused_body if mesh.shape["tp"] == 4 else plain_body
    return jax.shard_map(body, mesh=mesh, in_specs=in_specs, out_specs=out_specs, check_vma=False)
```

```python
import functools
import math

import jax
import jax.numpy as jnp
from jax import lax
from jax.experimental import pallas as pl
from jax.experimental.pallas import tpu as pltpu
from jax.sharding import PartitionSpec as P

HD = 128
QPK = 2


epsilon = 1e-06


def from_behind(block, axis, distance):
    devices = range(lax.axis_size(axis))
    route = [(i - distance, i) for i in devices if i - distance in devices]
    return lax.ppermute(block, axis, route)


def plain_body(
    teacher_hidden,
    proj_weight,
    student_in,
    norm_gain,
    w_query,
    w_keyval,
    w_out,
    row_offsets,
    row_counts,
    doc_start,
):
    scale = 1.0 / math.sqrt(HD)
    tokens_here = teacher_hidden.shape[0]
    quarter = tokens_here // 4
    slots_here = student_in.shape[0]
    width = student_in.shape[1]
    start = row_offsets[0] - lax.axis_index("seq") * tokens_here + quarter
    count = row_counts[0]
    xf = student_in.astype(jnp.float32)
    inv = lax.rsqrt(jnp.mean(xf * xf, axis=1, keepdims=True) + epsilon)
    normed = (xf * inv * norm_gain).astype(jnp.bfloat16)
    query = (
        jnp.dot(normed, w_query, preferred_element_type=jnp.float32)
        .astype(jnp.bfloat16)
        .reshape(slots_here, QPK, HD)
    )
    keyval = (
        jnp.dot(normed, w_keyval, preferred_element_type=jnp.float32)
        .astype(jnp.bfloat16)
        .reshape(slots_here, 2, HD)
    )
    keys = keyval[:, 0, :]
    values = keyval[:, 1, :]
    slots = jnp.arange(slots_here, dtype=jnp.int32)
    allowed = (slots[None, :] >= doc_start[:, None]) & (slots[None, :] <= slots[:, None])
    scores = jnp.einsum("peh,kh->epk", query, keys, preferred_element_type=jnp.float32) * scale
    scores = jnp.where(allowed[None], scores, -jnp.inf)
    top = jnp.max(scores, axis=-1, keepdims=True)
    expo = jnp.exp(scores - top)
    probs = expo / jnp.sum(expo, axis=-1, keepdims=True)
    probs_b = probs.astype(jnp.bfloat16)
    attn = jnp.einsum("epk,kh->peh", probs_b, values, preferred_element_type=jnp.float32).astype(
        jnp.bfloat16
    )
    attn = attn.reshape(slots_here, QPK * HD)
    branch_part = jnp.dot(attn, w_out, preferred_element_type=jnp.float32).astype(jnp.bfloat16)
    earlier = from_behind(teacher_hidden[tokens_here - quarter :], "seq", 1)
    features = jnp.concatenate(
        [earlier, teacher_hidden, jnp.zeros((quarter, teacher_hidden.shape[1]), jnp.bfloat16)],
        axis=0,
    )
    picked = lax.dynamic_slice_in_dim(features, start, slots_here, 0)
    projected = jnp.dot(picked, proj_weight, preferred_element_type=jnp.float32).astype(
        jnp.bfloat16
    )
    goal_sum, branch = (
        lax.psum(projected, "tp").astype(jnp.float32),
        lax.psum(branch_part, "tp").astype(jnp.float32),
    )
    goal = goal_sum.astype(jnp.bfloat16)
    student_out = (xf + branch).astype(jnp.bfloat16)
    yf = student_out.astype(jnp.float32)
    tf = goal.astype(jnp.float32)
    live = (slots < count).astype(jnp.float32)[:, None]
    asum = jnp.sum(yf * yf, axis=1, keepdims=True) + epsilon
    bsum = jnp.sum(tf * tf, axis=1, keepdims=True) + epsilon
    both = lax.rsqrt(asum * bsum)
    cosv = jnp.sum(yf * tf, axis=1, keepdims=True) * both
    dy = -math.sqrt(width) * live * (tf * both - cosv * yf / asum)
    dy_b = dy.astype(jnp.bfloat16)
    d_attn = lax.dot_general(
        dy_b, w_out, (((1,), (1,)), ((), ())), preferred_element_type=jnp.float32
    ).astype(jnp.bfloat16)
    d_out = d_attn.reshape(slots_here, QPK, HD)
    d_values = jnp.einsum("epk,peh->kh", probs_b, d_out, preferred_element_type=jnp.float32).astype(
        jnp.bfloat16
    )
    dprob = jnp.einsum("peh,kh->epk", d_out, values, preferred_element_type=jnp.float32)
    dscore = probs * (dprob - jnp.sum(dprob * probs, axis=-1, keepdims=True)) * scale
    dscore_b = dscore.astype(jnp.bfloat16)
    d_query = jnp.einsum("epk,kh->peh", dscore_b, keys, preferred_element_type=jnp.float32).astype(
        jnp.bfloat16
    )
    d_query = d_query.reshape(slots_here, QPK * HD)
    d_keys = jnp.einsum("epk,peh->kh", dscore_b, query, preferred_element_type=jnp.float32).astype(
        jnp.bfloat16
    )
    d_keyval = jnp.stack([d_keys, d_values], axis=1).reshape(slots_here, 2 * HD)
    own_rows = slots_here // lax.axis_size("tp")
    total = lax.dot_general(
        d_query, w_query, (((1,), (1,)), ((), ())), preferred_element_type=jnp.float32
    )
    d_normed = lax.psum_scatter(
        (
            total
            + lax.dot_general(
                d_keyval, w_keyval, (((1,), (1,)), ((), ())), preferred_element_type=jnp.float32
            )
        ).astype(jnp.bfloat16),
        "tp",
        scatter_dimension=0,
        tiled=True,
    ).astype(jnp.float32)
    first_row = lax.axis_index("tp") * own_rows
    x_own = lax.dynamic_slice_in_dim(xf, first_row, own_rows, 0)
    inv_own = lax.dynamic_slice_in_dim(inv, first_row, own_rows, 0)
    dy_own = lax.dynamic_slice_in_dim(dy, first_row, own_rows, 0)
    upper = d_normed * norm_gain
    dx = inv_own * upper - x_own * inv_own * inv_own * inv_own * jnp.mean(
        upper * x_own, axis=1, keepdims=True
    )
    grad_in = (dy_own + dx).astype(jnp.bfloat16)
    return (student_out, grad_in)


MESH = pl.DeviceIdType.MESH
NT = (((1,), (1,)), ((), ()))
TN = (((0,), (0,)), ((), ()))
F32 = jnp.float32
BF16 = jnp.bfloat16


def dot(a, b, dims=None):
    if dims is None:
        return jnp.dot(a, b, preferred_element_type=F32)
    return lax.dot_general(a, b, dims, preferred_element_type=F32)


def step_kernel(
    n_seq,
    offset_ref,
    count_ref,
    start_hbm,
    gain_hbm,
    teacher_hbm,
    proj_hbm,
    x_hbm,
    wq_hbm,
    wkv_hbm,
    wo_hbm,
    out_ref,
    grad_ref,
    start_s,
    gain_s,
    feat,
    proj,
    x_in,
    wq,
    wkv,
    wo,
    xq,
    normed,
    inv_s,
    qkv,
    probs_s,
    attn_s,
    g_part,
    g_near,
    g_chip,
    g_far,
    b_part,
    b_near,
    b_chip,
    b_far,
    t_s,
    y_s,
    dy_s,
    dy_own,
    d_attn_s,
    dd_s,
    n_part,
    n_near,
    n_chip,
    n_far,
    dn_s,
    load_sem,
    proj_sem,
    send_sem,
    recv_sem,
    shift_sem,
    out_sem,
):
    rows, width = x_in.shape
    quarter = rows // 4
    chunks, _, chunk = proj.shape
    own_tokens = teacher_hbm.shape[0]
    shift = rows - own_tokens
    s = lax.axis_index("seq")
    me = lax.axis_index("tp")
    c = lax.rem(me, 2)
    y = me // 2
    near = {"tp": y * 2 + 1 - c}
    far = {"tp": (1 - y) * 2 + c}
    scale = 1.0 / math.sqrt(HD)

    barrier = pltpu.get_barrier_semaphore()
    pl.semaphore_signal(barrier, inc=1, device_id=near, device_id_type=MESH)
    pl.semaphore_signal(barrier, inc=1, device_id=far, device_id_type=MESH)

    @pl.when(s > 0)
    def _():
        pl.semaphore_signal(barrier, inc=1, device_id={"seq": s - 1}, device_id_type=MESH)

    @pl.when(s < n_seq - 1)
    def _():
        pl.semaphore_signal(barrier, inc=1, device_id={"seq": s + 1}, device_id_type=MESH)

    def gain(k):
        return gain_s[cols(k)][None, :]

    def cols(k):
        return pl.ds(pl.multiple_of(k * chunk, chunk), chunk)

    loads = [
        pltpu.make_async_copy(a, b, load_sem.at[i])
        for i, (a, b) in enumerate(
            [
                (x_hbm, x_in),
                (wq_hbm, wq),
                (wkv_hbm, wkv),
                (teacher_hbm, feat.at[pl.ds(shift, own_tokens)]),
                (wo_hbm, wo),
                (start_hbm, start_s),
                (gain_hbm, gain_s),
            ]
        )
    ]
    for i in (0, 6, 3, 1):
        loads[i].start()

    def proj_load(k):
        return pltpu.make_async_copy(proj_hbm.at[:, cols(k)], proj.at[k], proj_sem.at[k])

    def start_proj(k, _):
        proj_load(k).start()
        return 0

    lax.fori_loop(0, chunks, start_proj, 0)
    for i in (2, 5, 4):
        loads[i].start()

    loads[0].wait()

    def square(k, acc):
        v = x_in[:, cols(k)].astype(F32)
        for q in range(4):
            xq[q % 2, q // 2, :, cols(k)] = v[q * quarter : (q + 1) * quarter]
        return acc + jnp.sum(v * v, axis=1, keepdims=True)

    total = lax.fori_loop(0, chunks, square, jnp.zeros((rows, 1), F32))
    inv = lax.rsqrt(total / width + epsilon)
    for q in range(4):
        inv_s[q] = inv[q * quarter : (q + 1) * quarter]

    inner = (s > 0) & (s < n_seq - 1)

    @pl.when(inner)
    def _():
        pl.semaphore_wait(barrier, 4)

    @pl.when(jnp.logical_not(inner))
    def _():
        pl.semaphore_wait(barrier, 3)

    def shift_copy(to):
        return pltpu.make_async_remote_copy(
            src_ref=teacher_hbm.at[pl.ds(own_tokens - shift, shift)],
            dst_ref=feat.at[pl.ds(0, shift)],
            send_sem=shift_sem.at[0],
            recv_sem=shift_sem.at[1],
            device_id={"seq": to},
            device_id_type=MESH,
        )

    @pl.when(s < n_seq - 1)
    def _():
        shift_copy(s + 1).start()

    @pl.when(s == 0)
    def _():
        feat[0:shift, :] = jnp.zeros((shift, feat.shape[1]), BF16)

    def remote(kind, k, src, dst, to):
        return pltpu.make_async_remote_copy(
            src_ref=src,
            dst_ref=dst,
            send_sem=send_sem.at[kind, k],
            recv_sem=recv_sem.at[kind, k],
            device_id=to,
            device_id_type=MESH,
        )

    def split_store(ref, k, val):
        for q in range(4):
            ref[k, q % 2, q // 2] = val[q * quarter : (q + 1) * quarter].astype(BF16)

    loads[6].wait()

    def norm(k, _):
        v = x_in[:, cols(k)].astype(F32)
        normed[:, cols(k)] = (v * inv * gain(k)).astype(BF16)
        return 0

    lax.fori_loop(0, chunks, norm, 0)

    loads[1].wait()
    qkv[:, 0 : QPK * HD] = dot(normed[...], wq[...]).astype(BF16)

    start = offset_ref[0] - s * own_tokens + shift
    r_i = lax.broadcasted_iota(jnp.int32, (rows, rows), 0)
    c_i = lax.broadcasted_iota(jnp.int32, (rows, rows), 1)

    @pl.when(s > 0)
    def _():
        shift_copy(s).wait_recv()

    loads[3].wait()
    select = jnp.where(c_i == r_i + start, 1.0, 0.0).astype(BF16)
    feat[...] = dot(select, feat[...]).astype(BF16)

    def near_copy(kind, k, part, land):
        return remote(kind, k, part.at[k, 1 - c], land.at[k], near)

    def far_copy(kind, k, chip, land):
        return remote(kind, k, chip.at[k], land.at[k], far)

    def pass_on(kind, k, part, land, chip, far_land):
        near_copy(kind, k, part, land).wait_recv()
        pair = part[k, c, 1 - y].astype(F32) + land[k, 1 - y].astype(F32)
        chip[k] = pair.astype(BF16)
        far_copy(kind + 1, k, chip, far_land).start()

    def own_sum(kind, k, part, land, chip, far_land):
        far_copy(kind + 1, k, chip, far_land).wait_recv()
        return (
            part[k, c, y].astype(F32) + land[k, y].astype(F32) + far_land[k].astype(F32)
        )

    lag = min(2, chunks)

    def scatter(kind, make, part, land, chip, far_land):
        def step(k, _):
            split_store(part, k, make(k))
            near_copy(kind, k, part, land).start()

            @pl.when(k >= lag)
            def _():
                pass_on(kind, k - lag, part, land, chip, far_land)

            return 0

        lax.fori_loop(0, chunks, step, 0)

    def scatter_rest(kind, part, land, chip, far_land):
        for k in range(chunks - lag, chunks):
            pass_on(kind, k, part, land, chip, far_land)

    def project(k):
        proj_load(k).wait()
        return dot(feat[...], proj[k])

    goal_bufs = (g_part, g_near, g_chip, g_far)
    scatter(0, project, *goal_bufs)
    loads[2].wait()
    scatter_rest(0, *goal_bufs)
    qkv[:, QPK * HD :] = dot(normed[...], wkv[...]).astype(BF16)
    loads[5].wait()

    starts = jnp.sum(
        jnp.where(r_i == c_i, start_s[...][None, :].astype(F32), 0.0), axis=1, keepdims=True
    )
    c_f = c_i.astype(F32)
    allowed = (c_f >= starts) & (c_i <= r_i)
    keys = qkv[:, QPK * HD : (QPK + 1) * HD]
    values = qkv[:, (QPK + 1) * HD :]
    for e in range(QPK):
        scores = dot(qkv[:, e * HD : (e + 1) * HD], keys, NT) * scale
        scores = jnp.where(allowed, scores, -jnp.inf)
        expo = jnp.exp(scores - jnp.max(scores, axis=-1, keepdims=True))
        probs = expo / jnp.sum(expo, axis=-1, keepdims=True)
        probs_s[e] = probs
        attn_s[:, e * HD : (e + 1) * HD] = dot(probs.astype(BF16), values).astype(BF16)

    loads[4].wait()

    branch_bufs = (b_part, b_near, b_chip, b_far)
    scatter(2, lambda k: dot(attn_s[...], wo[:, cols(k)]), *branch_bufs)
    scatter_rest(2, *branch_bufs)

    def y_copy(kind, k, owner, to):
        return remote(kind, k, y_s.at[k, c, owner], y_s.at[k, c, owner], to)

    def dy_copy(kind, k, owner, to):
        return remote(kind, k, dy_s.at[k, c, owner], dy_s.at[k, c, owner], to)

    def loss_step(k, sums):
        asum, bsum, both = sums
        t = own_sum(0, k, *goal_bufs).astype(BF16).astype(F32)
        t_s[k] = t
        out = (xq[c, y, :, cols(k)] + own_sum(2, k, *branch_bufs)).astype(BF16)
        y_s[k, c, y] = out
        y_copy(5, k, y, near).start()
        out = out.astype(F32)
        return (
            asum + jnp.sum(out * out, axis=-1, keepdims=True),
            bsum + jnp.sum(t * t, axis=-1, keepdims=True),
            both + jnp.sum(out * t, axis=-1, keepdims=True),
        )

    zero = jnp.zeros((quarter, 1), F32)
    asum, bsum, both_sum = lax.fori_loop(0, chunks, loss_step, (zero, zero, zero))
    early = min(3, chunks)

    def start_y(k, _):
        y_copy(4, k, y, far).start()
        return 0

    lax.fori_loop(0, early, start_y, 0)
    asum = asum + epsilon
    bsum = bsum + epsilon
    both = lax.rsqrt(asum * bsum)
    cosv = both_sum * both
    slot = lax.broadcasted_iota(jnp.int32, (quarter, 1), 0) + (2 * y + c) * quarter
    live = jnp.where(slot < count_ref[0], -math.sqrt(width), 0.0)
    t_factor = live * both
    y_factor = live * cosv / asum

    def dy_step(k, _):
        dy = t_s[k] * t_factor - y_s[k, c, y].astype(F32) * y_factor
        dy_s[k, c, y] = dy.astype(BF16)
        dy_copy(7, k, y, far).start()
        dy_copy(8, k, y, near).start()
        dy_own[:, cols(k)] = dy
        return 0

    lax.fori_loop(0, chunks, dy_step, 0)

    d_attn_s[...] = jnp.zeros_like(d_attn_s)

    def d_attn_part(k):
        dy_copy(8, k, y, near).wait_recv()
        dy_copy(9, k, 1 - y, near).wait_recv()
        dy = jnp.concatenate(
            [dy_s[k, q % 2, q // 2].astype(F32) for q in range(4)], axis=0
        ).astype(BF16)
        d_attn_s[...] += dot(dy, wo[:, cols(k)], NT)

    def d_attn_step(k, _):
        dy_copy(7, k, y, far).wait_recv()
        dy_copy(9, k, 1 - y, near).start()

        @pl.when(k > 0)
        def _():
            d_attn_part(k - 1)

        return 0

    lax.fori_loop(0, chunks, d_attn_step, 0)
    lax.fori_loop(early, chunks, start_y, 0)
    d_attn_part(chunks - 1)

    d_values = jnp.zeros((rows, HD), F32)
    d_keys = jnp.zeros((rows, HD), F32)
    for e in range(QPK):
        probs = probs_s[e]
        d_out = d_attn_s[:, e * HD : (e + 1) * HD].astype(BF16)
        d_values += dot(probs.astype(BF16), d_out, TN)
        dprob = dot(d_out, values, NT)
        dscore = probs * (dprob - jnp.sum(dprob * probs, axis=-1, keepdims=True)) * scale
        dscore_b = dscore.astype(BF16)
        dd_s[:, e * HD : (e + 1) * HD] = dot(dscore_b, keys).astype(BF16)
        d_keys += dot(dscore_b, qkv[:, e * HD : (e + 1) * HD], TN)
    dd_s[:, QPK * HD : (QPK + 1) * HD] = d_keys.astype(BF16)
    dd_s[:, (QPK + 1) * HD :] = d_values.astype(BF16)

    def d_normed(k):
        return dot(dd_s[:, 0 : QPK * HD], wq[cols(k), :], NT) + dot(
            dd_s[:, QPK * HD :], wkv[cols(k), :], NT
        )

    n_bufs = (n_part, n_near, n_chip, n_far)
    scatter(10, d_normed, *n_bufs)
    scatter_rest(10, *n_bufs)

    def forward_y(k, _):
        y_copy(4, k, y, far).wait_recv()
        y_copy(6, k, 1 - y, near).start()
        return 0

    lax.fori_loop(0, chunks, forward_y, 0)

    def out_copy(k, q):
        return pltpu.make_async_copy(
            y_s.at[k, q % 2, q // 2], out_ref.at[q, :, cols(k)], out_sem.at[k, q]
        )

    def out_step(k, _):
        y_copy(5, k, y, near).wait_recv()
        y_copy(6, k, 1 - y, near).wait_recv()
        for q in range(4):
            out_copy(k, q).start()
        return 0

    lax.fori_loop(0, chunks, out_step, 0)

    def drain_early(k, _):
        for kind, bufs in ((0, goal_bufs), (2, branch_bufs)):
            near_copy(kind, k, bufs[0], bufs[1]).wait_send()
            far_copy(kind + 1, k, bufs[2], bufs[3]).wait_send()
        for first, copy in ((4, y_copy), (7, dy_copy)):
            copy(first, k, y, far).wait_send()
            copy(first + 1, k, y, near).wait_send()
            copy(first + 2, k, 1 - y, near).wait_send()
        return 0

    lax.fori_loop(0, chunks, drain_early, 0)

    @pl.when(s < n_seq - 1)
    def _():
        shift_copy(s + 1).wait_send()

    def sum_step(k, acc):
        upper = own_sum(10, k, *n_bufs) * gain(k)
        dn_s[:, cols(k)] = upper
        return acc + jnp.sum(upper * xq[c, y, :, cols(k)], axis=-1, keepdims=True)

    acc = lax.fori_loop(0, chunks, sum_step, zero)
    inv_own = inv_s[y * 2 + c]
    x_factor = inv_own * inv_own * inv_own * (acc / width)

    def grad_step(k, _):
        dx = inv_own * dn_s[:, cols(k)] - xq[c, y, :, cols(k)] * x_factor
        grad_ref[:, cols(k)] = (dy_own[:, cols(k)] + dx).astype(BF16)
        return 0

    lax.fori_loop(0, chunks, grad_step, 0)

    def drain(k, _):
        for q in range(4):
            out_copy(k, q).wait()
        near_copy(10, k, n_part, n_near).wait_send()
        far_copy(11, k, n_chip, n_far).wait_send()
        return 0

    lax.fori_loop(0, chunks, drain, 0)


def hand_over(y_ref, g_ref, out_ref, grad_ref, y_buf, g_buf, in_sem, out_sem):
    spans = [(y_ref.at[q], y_buf.at[q], out_ref.at[q]) for q in range(4)]
    spans.append((g_ref, g_buf, grad_ref))
    inward = [pltpu.make_async_copy(a, b, in_sem.at[i]) for i, (a, b, _) in enumerate(spans)]
    outward = [pltpu.make_async_copy(b, a, out_sem.at[i]) for i, (_, b, a) in enumerate(spans)]
    for one in inward:
        one.start()
    for one, then in zip(inward, outward):
        one.wait()
        then.start()
    for one in outward:
        one.wait()


def chunk_of(width):
    for size in (512, 256, 128):
        if width % size == 0:
            return size
    return width


def fused_body(
    teacher_hidden,
    proj_weight,
    student_in,
    norm_gain,
    w_query,
    w_keyval,
    w_out,
    row_offsets,
    row_counts,
    doc_start,
):
    rows, width = student_in.shape
    depth = teacher_hidden.shape[1]
    heads = w_query.shape[1]
    quarter = rows // 4
    chunk = chunk_of(width)
    k = width // chunk
    vmem = pltpu.VMEM
    half = (k, 2, quarter, chunk)
    parts = (k, 2, 2, quarter, chunk)
    own = (k, quarter, chunk)
    scratch = [
        vmem((rows,), jnp.int32),
        vmem((width,), F32),
        vmem((rows, depth), BF16),
        vmem((k, depth, chunk), BF16),
        vmem((rows, width), BF16),
        vmem(w_query.shape, BF16),
        vmem(w_keyval.shape, BF16),
        vmem(w_out.shape, BF16),
        vmem((2, 2, quarter, width), F32),
        vmem((rows, width), BF16),
        vmem((4, quarter, 1), F32),
        vmem((rows, 2 * heads), BF16),
        vmem((QPK, rows, rows), F32),
        vmem((rows, heads), BF16),
        vmem(parts, BF16),
        vmem(half, BF16),
        vmem(own, BF16),
        vmem(own, BF16),
        vmem(parts, BF16),
        vmem(half, BF16),
        vmem(own, BF16),
        vmem(own, BF16),
        vmem(own, F32),
        vmem(parts, BF16),
        vmem(parts, BF16),
        vmem((quarter, width), F32),
        vmem((rows, heads), F32),
        vmem((rows, 2 * heads), BF16),
        vmem(parts, BF16),
        vmem(half, BF16),
        vmem(own, BF16),
        vmem(own, BF16),
        vmem((quarter, width), F32),
        pltpu.SemaphoreType.DMA((7,)),
        pltpu.SemaphoreType.DMA((k,)),
        pltpu.SemaphoreType.DMA((12, k)),
        pltpu.SemaphoreType.DMA((12, k)),
        pltpu.SemaphoreType.DMA((2,)),
        pltpu.SemaphoreType.DMA((k, 4)),
    ]
    smem = pl.BlockSpec(memory_space=pltpu.SMEM)
    in_vmem = pl.BlockSpec(memory_space=pltpu.VMEM)
    in_hbm = pl.BlockSpec(memory_space=pltpu.HBM)
    flops = 2 * rows * width * (depth + 6 * heads)
    moved = 2 * width * (depth + 3 * heads + 3 * rows)
    student_out, grad_in = pl.pallas_call(
        functools.partial(step_kernel, lax.axis_size("seq")),
        out_shape=(
            jax.ShapeDtypeStruct((4, quarter, width), BF16),
            jax.ShapeDtypeStruct((quarter, width), BF16),
        ),
        in_specs=[smem, smem] + [in_hbm] * 8,
        out_specs=(in_hbm, in_vmem),
        scratch_shapes=scratch,
        cost_estimate=pl.CostEstimate(flops=flops, bytes_accessed=moved, transcendentals=0),
        compiler_params=pltpu.CompilerParams(
            collective_id=0, has_side_effects=True, vmem_limit_bytes=VMEM_BYTES
        ),
    )(
        row_offsets,
        row_counts,
        doc_start,
        norm_gain,
        teacher_hidden,
        proj_weight,
        student_in,
        w_query,
        w_keyval,
        w_out,
    )
    student_out, grad_in = pl.pallas_call(
        hand_over,
        out_shape=(
            jax.ShapeDtypeStruct(student_out.shape, BF16),
            jax.ShapeDtypeStruct(grad_in.shape, BF16),
        ),
        in_specs=[in_hbm, in_hbm],
        out_specs=(in_hbm, in_hbm),
        scratch_shapes=[
            vmem(student_out.shape, BF16),
            vmem(grad_in.shape, BF16),
            pltpu.SemaphoreType.DMA((5,)),
            pltpu.SemaphoreType.DMA((5,)),
        ],
        compiler_params=pltpu.CompilerParams(vmem_limit_bytes=VMEM_BYTES),
    )(student_out, grad_in)
    return (student_out.reshape(rows, width), grad_in)


VMEM_BYTES = 60 * 2**20


def solution(mesh):
    in_specs = (
        P("seq", "tp"),
        P("tp", None),
        P("seq", None),
        P(),
        P(None, "tp"),
        P(None, "tp"),
        P("tp", None),
        P("seq"),
        P("seq"),
        P("seq"),
    )
    out_specs = (P("seq", None), P(("seq", "tp"), None))
    body = fused_body if mesh.shape["tp"] == 4 else plain_body
    return jax.shard_map(body, mesh=mesh, in_specs=in_specs, out_specs=out_specs, check_vma=False)
```

```python
import functools
import math

import jax
import jax.numpy as jnp
from jax import lax
from jax.experimental import pallas as pl
from jax.experimental.pallas import tpu as pltpu
from jax.sharding import PartitionSpec as P

HD = 128
QPK = 2


epsilon = 1e-06


def from_behind(block, axis, distance):
    devices = range(lax.axis_size(axis))
    route = [(i - distance, i) for i in devices if i - distance in devices]
    return lax.ppermute(block, axis, route)


def plain_body(
    teacher_hidden,
    proj_weight,
    student_in,
    norm_gain,
    w_query,
    w_keyval,
    w_out,
    row_offsets,
    row_counts,
    doc_start,
):
    scale = 1.0 / math.sqrt(HD)
    tokens_here = teacher_hidden.shape[0]
    quarter = tokens_here // 4
    slots_here = student_in.shape[0]
    width = student_in.shape[1]
    start = row_offsets[0] - lax.axis_index("seq") * tokens_here + quarter
    count = row_counts[0]
    xf = student_in.astype(jnp.float32)
    inv = lax.rsqrt(jnp.mean(xf * xf, axis=1, keepdims=True) + epsilon)
    normed = (xf * inv * norm_gain).astype(jnp.bfloat16)
    query = (
        jnp.dot(normed, w_query, preferred_element_type=jnp.float32)
        .astype(jnp.bfloat16)
        .reshape(slots_here, QPK, HD)
    )
    keyval = (
        jnp.dot(normed, w_keyval, preferred_element_type=jnp.float32)
        .astype(jnp.bfloat16)
        .reshape(slots_here, 2, HD)
    )
    keys = keyval[:, 0, :]
    values = keyval[:, 1, :]
    slots = jnp.arange(slots_here, dtype=jnp.int32)
    allowed = (slots[None, :] >= doc_start[:, None]) & (slots[None, :] <= slots[:, None])
    scores = jnp.einsum("peh,kh->epk", query, keys, preferred_element_type=jnp.float32) * scale
    scores = jnp.where(allowed[None], scores, -jnp.inf)
    top = jnp.max(scores, axis=-1, keepdims=True)
    expo = jnp.exp(scores - top)
    probs = expo / jnp.sum(expo, axis=-1, keepdims=True)
    probs_b = probs.astype(jnp.bfloat16)
    attn = jnp.einsum("epk,kh->peh", probs_b, values, preferred_element_type=jnp.float32).astype(
        jnp.bfloat16
    )
    attn = attn.reshape(slots_here, QPK * HD)
    branch_part = jnp.dot(attn, w_out, preferred_element_type=jnp.float32).astype(jnp.bfloat16)
    earlier = from_behind(teacher_hidden[tokens_here - quarter :], "seq", 1)
    features = jnp.concatenate(
        [earlier, teacher_hidden, jnp.zeros((quarter, teacher_hidden.shape[1]), jnp.bfloat16)],
        axis=0,
    )
    picked = lax.dynamic_slice_in_dim(features, start, slots_here, 0)
    projected = jnp.dot(picked, proj_weight, preferred_element_type=jnp.float32).astype(
        jnp.bfloat16
    )
    goal_sum, branch = (
        lax.psum(projected, "tp").astype(jnp.float32),
        lax.psum(branch_part, "tp").astype(jnp.float32),
    )
    goal = goal_sum.astype(jnp.bfloat16)
    student_out = (xf + branch).astype(jnp.bfloat16)
    yf = student_out.astype(jnp.float32)
    tf = goal.astype(jnp.float32)
    live = (slots < count).astype(jnp.float32)[:, None]
    asum = jnp.sum(yf * yf, axis=1, keepdims=True) + epsilon
    bsum = jnp.sum(tf * tf, axis=1, keepdims=True) + epsilon
    both = lax.rsqrt(asum * bsum)
    cosv = jnp.sum(yf * tf, axis=1, keepdims=True) * both
    dy = -math.sqrt(width) * live * (tf * both - cosv * yf / asum)
    dy_b = dy.astype(jnp.bfloat16)
    d_attn = lax.dot_general(
        dy_b, w_out, (((1,), (1,)), ((), ())), preferred_element_type=jnp.float32
    ).astype(jnp.bfloat16)
    d_out = d_attn.reshape(slots_here, QPK, HD)
    d_values = jnp.einsum("epk,peh->kh", probs_b, d_out, preferred_element_type=jnp.float32).astype(
        jnp.bfloat16
    )
    dprob = jnp.einsum("peh,kh->epk", d_out, values, preferred_element_type=jnp.float32)
    dscore = probs * (dprob - jnp.sum(dprob * probs, axis=-1, keepdims=True)) * scale
    dscore_b = dscore.astype(jnp.bfloat16)
    d_query = jnp.einsum("epk,kh->peh", dscore_b, keys, preferred_element_type=jnp.float32).astype(
        jnp.bfloat16
    )
    d_query = d_query.reshape(slots_here, QPK * HD)
    d_keys = jnp.einsum("epk,peh->kh", dscore_b, query, preferred_element_type=jnp.float32).astype(
        jnp.bfloat16
    )
    d_keyval = jnp.stack([d_keys, d_values], axis=1).reshape(slots_here, 2 * HD)
    own_rows = slots_here // lax.axis_size("tp")
    total = lax.dot_general(
        d_query, w_query, (((1,), (1,)), ((), ())), preferred_element_type=jnp.float32
    )
    d_normed = lax.psum_scatter(
        (
            total
            + lax.dot_general(
                d_keyval, w_keyval, (((1,), (1,)), ((), ())), preferred_element_type=jnp.float32
            )
        ).astype(jnp.bfloat16),
        "tp",
        scatter_dimension=0,
        tiled=True,
    ).astype(jnp.float32)
    first_row = lax.axis_index("tp") * own_rows
    x_own = lax.dynamic_slice_in_dim(xf, first_row, own_rows, 0)
    inv_own = lax.dynamic_slice_in_dim(inv, first_row, own_rows, 0)
    dy_own = lax.dynamic_slice_in_dim(dy, first_row, own_rows, 0)
    upper = d_normed * norm_gain
    dx = inv_own * upper - x_own * inv_own * inv_own * inv_own * jnp.mean(
        upper * x_own, axis=1, keepdims=True
    )
    grad_in = (dy_own + dx).astype(jnp.bfloat16)
    return (student_out, grad_in)


MESH = pl.DeviceIdType.MESH


def unrolled(count, step, carry):
    for k in range(count):
        carry = step(k, carry)
    return carry


NT = (((1,), (1,)), ((), ()))
TN = (((0,), (0,)), ((), ()))
F32 = jnp.float32
BF16 = jnp.bfloat16


def dot(a, b, dims=None):
    if dims is None:
        return jnp.dot(a, b, preferred_element_type=F32)
    return lax.dot_general(a, b, dims, preferred_element_type=F32)


def step_kernel(
    n_seq,
    offset_ref,
    count_ref,
    start_hbm,
    gain_hbm,
    teacher_hbm,
    proj_hbm,
    x_hbm,
    wq_hbm,
    wkv_hbm,
    wo_hbm,
    out_ref,
    grad_ref,
    start_s,
    gain_s,
    feat,
    proj,
    x_in,
    wq,
    wkv,
    wo,
    xq,
    normed,
    inv_s,
    qkv,
    probs_s,
    attn_s,
    g_part,
    g_near,
    g_chip,
    g_far,
    b_part,
    b_near,
    b_chip,
    b_far,
    t_s,
    y_s,
    dy_s,
    dy_own,
    d_attn_s,
    dd_s,
    n_part,
    n_near,
    n_chip,
    n_far,
    dn_s,
    load_sem,
    proj_sem,
    send_sem,
    recv_sem,
    shift_sem,
    out_sem,
):
    rows, width = x_in.shape
    quarter = rows // 4
    chunks, _, chunk = proj.shape
    own_tokens = teacher_hbm.shape[0]
    shift = rows - own_tokens
    s = lax.axis_index("seq")
    me = lax.axis_index("tp")
    c = lax.rem(me, 2)
    y = me // 2
    near = {"tp": y * 2 + 1 - c}
    far = {"tp": (1 - y) * 2 + c}
    scale = 1.0 / math.sqrt(HD)

    barrier = pltpu.get_barrier_semaphore()
    pl.semaphore_signal(barrier, inc=1, device_id=near, device_id_type=MESH)
    pl.semaphore_signal(barrier, inc=1, device_id=far, device_id_type=MESH)

    @pl.when(s > 0)
    def _():
        pl.semaphore_signal(barrier, inc=1, device_id={"seq": s - 1}, device_id_type=MESH)

    @pl.when(s < n_seq - 1)
    def _():
        pl.semaphore_signal(barrier, inc=1, device_id={"seq": s + 1}, device_id_type=MESH)

    def gain(k):
        return gain_s[cols(k)][None, :]

    def cols(k):
        if isinstance(k, int):
            return pl.ds(k * chunk, chunk)
        return pl.ds(pl.multiple_of(k * chunk, chunk), chunk)

    loads = [
        pltpu.make_async_copy(a, b, load_sem.at[i])
        for i, (a, b) in enumerate(
            [
                (x_hbm, x_in),
                (wq_hbm, wq),
                (wkv_hbm, wkv),
                (teacher_hbm, feat.at[pl.ds(shift, own_tokens)]),
                (wo_hbm, wo),
                (start_hbm, start_s),
                (gain_hbm, gain_s),
            ]
        )
    ]
    for i in (0, 6, 3, 1):
        loads[i].start()

    def proj_load(k):
        return pltpu.make_async_copy(proj_hbm.at[:, cols(k)], proj.at[k], proj_sem.at[k])

    def start_proj(k, _):
        proj_load(k).start()
        return 0

    lax.fori_loop(0, chunks, start_proj, 0)
    for i in (2, 5, 4):
        loads[i].start()

    loads[0].wait()

    def square(k, acc):
        v = x_in[:, cols(k)].astype(F32)
        for q in range(4):
            xq[q % 2, q // 2, :, cols(k)] = v[q * quarter : (q + 1) * quarter]
        return acc + jnp.sum(v * v, axis=1, keepdims=True)

    total = unrolled(chunks, square, jnp.zeros((rows, 1), F32))
    inv = lax.rsqrt(total / width + epsilon)
    for q in range(4):
        inv_s[q] = inv[q * quarter : (q + 1) * quarter]

    inner = (s > 0) & (s < n_seq - 1)

    @pl.when(inner)
    def _():
        pl.semaphore_wait(barrier, 4)

    @pl.when(jnp.logical_not(inner))
    def _():
        pl.semaphore_wait(barrier, 3)

    def shift_copy(to):
        return pltpu.make_async_remote_copy(
            src_ref=teacher_hbm.at[pl.ds(own_tokens - shift, shift)],
            dst_ref=feat.at[pl.ds(0, shift)],
            send_sem=shift_sem.at[0],
            recv_sem=shift_sem.at[1],
            device_id={"seq": to},
            device_id_type=MESH,
        )

    @pl.when(s < n_seq - 1)
    def _():
        shift_copy(s + 1).start()

    @pl.when(s == 0)
    def _():
        feat[0:shift, :] = jnp.zeros((shift, feat.shape[1]), BF16)

    def remote(kind, k, src, dst, to):
        return pltpu.make_async_remote_copy(
            src_ref=src,
            dst_ref=dst,
            send_sem=send_sem.at[kind, k],
            recv_sem=recv_sem.at[kind, k],
            device_id=to,
            device_id_type=MESH,
        )

    def split_store(ref, k, val):
        for q in range(4):
            ref[k, q % 2, q // 2] = val[q * quarter : (q + 1) * quarter].astype(BF16)

    loads[6].wait()

    def norm(k, _):
        v = x_in[:, cols(k)].astype(F32)
        normed[:, cols(k)] = (v * inv * gain(k)).astype(BF16)
        return 0

    unrolled(chunks, norm, 0)

    loads[1].wait()
    qkv[:, 0 : QPK * HD] = dot(normed[...], wq[...]).astype(BF16)

    start = offset_ref[0] - s * own_tokens + shift
    r_i = lax.broadcasted_iota(jnp.int32, (rows, rows), 0)
    c_i = lax.broadcasted_iota(jnp.int32, (rows, rows), 1)

    @pl.when(s > 0)
    def _():
        shift_copy(s).wait_recv()

    loads[3].wait()
    select = jnp.where(c_i == r_i + start, 1.0, 0.0).astype(BF16)
    feat[...] = dot(select, feat[...]).astype(BF16)

    def near_copy(kind, k, part, land):
        return remote(kind, k, part.at[k, 1 - c], land.at[k], near)

    def far_copy(kind, k, chip, land):
        return remote(kind, k, chip.at[k], land.at[k], far)

    def add_pair(k, part, land, chip):
        pair = part[k, c, 1 - y].astype(F32) + land[k, 1 - y].astype(F32)
        chip[k] = pair.astype(BF16)

    def pass_on(kind, k, part, land, chip, far_land):
        near_copy(kind, k, part, land).wait_recv()
        add_pair(k, part, land, chip)
        far_copy(kind + 1, k, chip, far_land).start()

    def own_sum(kind, k, part, land, chip, far_land):
        far_copy(kind + 1, k, chip, far_land).wait_recv()
        return (
            part[k, c, y].astype(F32) + land[k, y].astype(F32) + far_land[k].astype(F32)
        )

    lag = min(2, chunks)

    def scatter(kind, make, part, land, chip, far_land):
        for k in range(chunks):
            behind = k - lag
            if behind >= 0:
                near_copy(kind, behind, part, land).wait_recv()
            val = make(k)
            if behind >= 0:
                add_pair(behind, part, land, chip)
            split_store(part, k, val)
            near_copy(kind, k, part, land).start()
            if behind >= 0:
                far_copy(kind + 1, behind, chip, far_land).start()

    def scatter_rest(kind, part, land, chip, far_land):
        for k in range(chunks - lag, chunks):
            pass_on(kind, k, part, land, chip, far_land)

    def project(k):
        proj_load(k).wait()
        return dot(feat[...], proj[k])

    goal_bufs = (g_part, g_near, g_chip, g_far)
    scatter(0, project, *goal_bufs)
    loads[2].wait()
    scatter_rest(0, *goal_bufs)
    qkv[:, QPK * HD :] = dot(normed[...], wkv[...]).astype(BF16)
    loads[5].wait()

    starts = jnp.sum(
        jnp.where(r_i == c_i, start_s[...][None, :].astype(F32), 0.0), axis=1, keepdims=True
    )
    c_f = c_i.astype(F32)
    allowed = (c_f >= starts) & (c_i <= r_i)
    keys = qkv[:, QPK * HD : (QPK + 1) * HD]
    values = qkv[:, (QPK + 1) * HD :]
    for e in range(QPK):
        scores = dot(qkv[:, e * HD : (e + 1) * HD], keys, NT) * scale
        scores = jnp.where(allowed, scores, -jnp.inf)
        expo = jnp.exp(scores - jnp.max(scores, axis=-1, keepdims=True))
        probs = expo / jnp.sum(expo, axis=-1, keepdims=True)
        probs_s[e] = probs
        attn_s[:, e * HD : (e + 1) * HD] = dot(probs.astype(BF16), values).astype(BF16)

    loads[4].wait()

    branch_bufs = (b_part, b_near, b_chip, b_far)
    scatter(2, lambda k: dot(attn_s[...], wo[:, cols(k)]), *branch_bufs)
    scatter_rest(2, *branch_bufs)

    def y_copy(kind, k, owner, to):
        return remote(kind, k, y_s.at[k, c, owner], y_s.at[k, c, owner], to)

    def dy_copy(kind, k, owner, to):
        return remote(kind, k, dy_s.at[k, c, owner], dy_s.at[k, c, owner], to)

    def loss_step(k, sums):
        asum, bsum, both = sums
        t = own_sum(0, k, *goal_bufs).astype(BF16).astype(F32)
        t_s[k] = t
        out = (xq[c, y, :, cols(k)] + own_sum(2, k, *branch_bufs)).astype(BF16)
        y_s[k, c, y] = out
        y_copy(5, k, y, near).start()
        out = out.astype(F32)
        return (
            asum + jnp.sum(out * out, axis=-1, keepdims=True),
            bsum + jnp.sum(t * t, axis=-1, keepdims=True),
            both + jnp.sum(out * t, axis=-1, keepdims=True),
        )

    zero = jnp.zeros((quarter, 1), F32)
    asum, bsum, both_sum = unrolled(chunks, loss_step, (zero, zero, zero))
    early = min(3, chunks)

    def start_y(k, _):
        y_copy(4, k, y, far).start()
        return 0

    lax.fori_loop(0, early, start_y, 0)
    asum = asum + epsilon
    bsum = bsum + epsilon
    both = lax.rsqrt(asum * bsum)
    cosv = both_sum * both
    slot = lax.broadcasted_iota(jnp.int32, (quarter, 1), 0) + (2 * y + c) * quarter
    live = jnp.where(slot < count_ref[0], -math.sqrt(width), 0.0)
    t_factor = live * both
    y_factor = live * cosv / asum

    def dy_step(k, _):
        dy = t_s[k] * t_factor - y_s[k, c, y].astype(F32) * y_factor
        dy_s[k, c, y] = dy.astype(BF16)
        dy_copy(7, k, y, far).start()
        dy_copy(8, k, y, near).start()
        dy_own[:, cols(k)] = dy
        return 0

    unrolled(chunks, dy_step, 0)

    d_attn_s[...] = jnp.zeros_like(d_attn_s)

    def d_attn_part(k):
        dy_copy(8, k, y, near).wait_recv()
        dy_copy(9, k, 1 - y, near).wait_recv()
        dy = jnp.concatenate(
            [dy_s[k, q % 2, q // 2].astype(F32) for q in range(4)], axis=0
        ).astype(BF16)
        d_attn_s[...] += dot(dy, wo[:, cols(k)], NT)

    def d_attn_step(k, _):
        dy_copy(7, k, y, far).wait_recv()
        dy_copy(9, k, 1 - y, near).start()

        if k > 0:
            d_attn_part(k - 1)

        return 0

    unrolled(chunks, d_attn_step, 0)
    lax.fori_loop(early, chunks, start_y, 0)
    d_attn_part(chunks - 1)

    d_values = jnp.zeros((rows, HD), F32)
    d_keys = jnp.zeros((rows, HD), F32)
    for e in range(QPK):
        probs = probs_s[e]
        d_out = d_attn_s[:, e * HD : (e + 1) * HD].astype(BF16)
        d_values += dot(probs.astype(BF16), d_out, TN)
        dprob = dot(d_out, values, NT)
        dscore = probs * (dprob - jnp.sum(dprob * probs, axis=-1, keepdims=True)) * scale
        dscore_b = dscore.astype(BF16)
        dd_s[:, e * HD : (e + 1) * HD] = dot(dscore_b, keys).astype(BF16)
        d_keys += dot(dscore_b, qkv[:, e * HD : (e + 1) * HD], TN)
    dd_s[:, QPK * HD : (QPK + 1) * HD] = d_keys.astype(BF16)
    dd_s[:, (QPK + 1) * HD :] = d_values.astype(BF16)

    def d_normed(k):
        return dot(dd_s[:, 0 : QPK * HD], wq[cols(k), :], NT) + dot(
            dd_s[:, QPK * HD :], wkv[cols(k), :], NT
        )

    n_bufs = (n_part, n_near, n_chip, n_far)
    scatter(10, d_normed, *n_bufs)
    scatter_rest(10, *n_bufs)

    def forward_y(k, _):
        y_copy(4, k, y, far).wait_recv()
        y_copy(6, k, 1 - y, near).start()
        return 0

    lax.fori_loop(0, chunks, forward_y, 0)

    def out_copy(k, q):
        return pltpu.make_async_copy(
            y_s.at[k, q % 2, q // 2], out_ref.at[q, :, cols(k)], out_sem.at[k, q]
        )

    def out_step(k, _):
        y_copy(5, k, y, near).wait_recv()
        y_copy(6, k, 1 - y, near).wait_recv()
        for q in range(4):
            out_copy(k, q).start()
        return 0

    lax.fori_loop(0, chunks, out_step, 0)

    def drain_early(k, _):
        for kind, bufs in ((0, goal_bufs), (2, branch_bufs)):
            near_copy(kind, k, bufs[0], bufs[1]).wait_send()
            far_copy(kind + 1, k, bufs[2], bufs[3]).wait_send()
        for first, copy in ((4, y_copy), (7, dy_copy)):
            copy(first, k, y, far).wait_send()
            copy(first + 1, k, y, near).wait_send()
            copy(first + 2, k, 1 - y, near).wait_send()
        return 0

    lax.fori_loop(0, chunks, drain_early, 0)

    @pl.when(s < n_seq - 1)
    def _():
        shift_copy(s + 1).wait_send()

    def sum_step(k, acc):
        upper = own_sum(10, k, *n_bufs) * gain(k)
        dn_s[:, cols(k)] = upper
        return acc + jnp.sum(upper * xq[c, y, :, cols(k)], axis=-1, keepdims=True)

    acc = unrolled(chunks, sum_step, zero)
    inv_own = inv_s[y * 2 + c]
    x_factor = inv_own * inv_own * inv_own * (acc / width)

    def grad_step(k, _):
        dx = inv_own * dn_s[:, cols(k)] - xq[c, y, :, cols(k)] * x_factor
        grad_ref[:, cols(k)] = (dy_own[:, cols(k)] + dx).astype(BF16)
        return 0

    unrolled(chunks, grad_step, 0)

    def drain(k, _):
        for q in range(4):
            out_copy(k, q).wait()
        near_copy(10, k, n_part, n_near).wait_send()
        far_copy(11, k, n_chip, n_far).wait_send()
        return 0

    lax.fori_loop(0, chunks, drain, 0)


def hand_over(y_ref, g_ref, out_ref, grad_ref, y_buf, g_buf, in_sem, out_sem):
    spans = [(y_ref.at[q], y_buf.at[q], out_ref.at[q]) for q in range(4)]
    spans.append((g_ref, g_buf, grad_ref))
    inward = [pltpu.make_async_copy(a, b, in_sem.at[i]) for i, (a, b, _) in enumerate(spans)]
    outward = [pltpu.make_async_copy(b, a, out_sem.at[i]) for i, (_, b, a) in enumerate(spans)]
    for one in inward:
        one.start()
    for one, then in zip(inward, outward):
        one.wait()
        then.start()
    for one in outward:
        one.wait()


def chunk_of(width):
    for size in (512, 256, 128):
        if width % size == 0:
            return size
    return width


def fused_body(
    teacher_hidden,
    proj_weight,
    student_in,
    norm_gain,
    w_query,
    w_keyval,
    w_out,
    row_offsets,
    row_counts,
    doc_start,
):
    rows, width = student_in.shape
    depth = teacher_hidden.shape[1]
    heads = w_query.shape[1]
    quarter = rows // 4
    chunk = chunk_of(width)
    k = width // chunk
    vmem = pltpu.VMEM
    half = (k, 2, quarter, chunk)
    parts = (k, 2, 2, quarter, chunk)
    own = (k, quarter, chunk)
    scratch = [
        vmem((rows,), jnp.int32),
        vmem((width,), F32),
        vmem((rows, depth), BF16),
        vmem((k, depth, chunk), BF16),
        vmem((rows, width), BF16),
        vmem(w_query.shape, BF16),
        vmem(w_keyval.shape, BF16),
        vmem(w_out.shape, BF16),
        vmem((2, 2, quarter, width), F32),
        vmem((rows, width), BF16),
        vmem((4, quarter, 1), F32),
        vmem((rows, 2 * heads), BF16),
        vmem((QPK, rows, rows), F32),
        vmem((rows, heads), BF16),
        vmem(parts, BF16),
        vmem(half, BF16),
        vmem(own, BF16),
        vmem(own, BF16),
        vmem(parts, BF16),
        vmem(half, BF16),
        vmem(own, BF16),
        vmem(own, BF16),
        vmem(own, F32),
        vmem(parts, BF16),
        vmem(parts, BF16),
        vmem((quarter, width), F32),
        vmem((rows, heads), F32),
        vmem((rows, 2 * heads), BF16),
        vmem(parts, BF16),
        vmem(half, BF16),
        vmem(own, BF16),
        vmem(own, BF16),
        vmem((quarter, width), F32),
        pltpu.SemaphoreType.DMA((7,)),
        pltpu.SemaphoreType.DMA((k,)),
        pltpu.SemaphoreType.DMA((12, k)),
        pltpu.SemaphoreType.DMA((12, k)),
        pltpu.SemaphoreType.DMA((2,)),
        pltpu.SemaphoreType.DMA((k, 4)),
    ]
    smem = pl.BlockSpec(memory_space=pltpu.SMEM)
    in_vmem = pl.BlockSpec(memory_space=pltpu.VMEM)
    in_hbm = pl.BlockSpec(memory_space=pltpu.HBM)
    flops = 2 * rows * width * (depth + 6 * heads)
    moved = 2 * width * (depth + 3 * heads + 3 * rows)
    student_out, grad_in = pl.pallas_call(
        functools.partial(step_kernel, lax.axis_size("seq")),
        out_shape=(
            jax.ShapeDtypeStruct((4, quarter, width), BF16),
            jax.ShapeDtypeStruct((quarter, width), BF16),
        ),
        in_specs=[smem, smem] + [in_hbm] * 8,
        out_specs=(in_hbm, in_vmem),
        scratch_shapes=scratch,
        cost_estimate=pl.CostEstimate(flops=flops, bytes_accessed=moved, transcendentals=0),
        compiler_params=pltpu.CompilerParams(
            collective_id=0, has_side_effects=True, vmem_limit_bytes=VMEM_BYTES
        ),
    )(
        row_offsets,
        row_counts,
        doc_start,
        norm_gain,
        teacher_hidden,
        proj_weight,
        student_in,
        w_query,
        w_keyval,
        w_out,
    )
    student_out, grad_in = pl.pallas_call(
        hand_over,
        out_shape=(
            jax.ShapeDtypeStruct(student_out.shape, BF16),
            jax.ShapeDtypeStruct(grad_in.shape, BF16),
        ),
        in_specs=[in_hbm, in_hbm],
        out_specs=(in_hbm, in_hbm),
        scratch_shapes=[
            vmem(student_out.shape, BF16),
            vmem(grad_in.shape, BF16),
            pltpu.SemaphoreType.DMA((5,)),
            pltpu.SemaphoreType.DMA((5,)),
        ],
        compiler_params=pltpu.CompilerParams(vmem_limit_bytes=VMEM_BYTES),
    )(student_out, grad_in)
    return (student_out.reshape(rows, width), grad_in)


VMEM_BYTES = 60 * 2**20


def solution(mesh):
    in_specs = (
        P("seq", "tp"),
        P("tp", None),
        P("seq", None),
        P(),
        P(None, "tp"),
        P(None, "tp"),
        P("tp", None),
        P("seq"),
        P("seq"),
        P("seq"),
    )
    out_specs = (P("seq", None), P(("seq", "tp"), None))
    body = fused_body if mesh.shape["tp"] == 4 else plain_body
    return jax.shard_map(body, mesh=mesh, in_specs=in_specs, out_specs=out_specs, check_vma=False)
```

```python
import functools
import math

import jax
import jax.numpy as jnp
from jax import lax
from jax.experimental import pallas as pl
from jax.experimental.pallas import tpu as pltpu
from jax.sharding import PartitionSpec as P

HD = 128
QPK = 2


epsilon = 1e-06


def from_behind(block, axis, distance):
    devices = range(lax.axis_size(axis))
    route = [(i - distance, i) for i in devices if i - distance in devices]
    return lax.ppermute(block, axis, route)


def plain_body(
    teacher_hidden,
    proj_weight,
    student_in,
    norm_gain,
    w_query,
    w_keyval,
    w_out,
    row_offsets,
    row_counts,
    doc_start,
):
    scale = 1.0 / math.sqrt(HD)
    tokens_here = teacher_hidden.shape[0]
    quarter = tokens_here // 4
    slots_here = student_in.shape[0]
    width = student_in.shape[1]
    start = row_offsets[0] - lax.axis_index("seq") * tokens_here + quarter
    count = row_counts[0]
    xf = student_in.astype(jnp.float32)
    inv = lax.rsqrt(jnp.mean(xf * xf, axis=1, keepdims=True) + epsilon)
    normed = (xf * inv * norm_gain).astype(jnp.bfloat16)
    query = (
        jnp.dot(normed, w_query, preferred_element_type=jnp.float32)
        .astype(jnp.bfloat16)
        .reshape(slots_here, QPK, HD)
    )
    keyval = (
        jnp.dot(normed, w_keyval, preferred_element_type=jnp.float32)
        .astype(jnp.bfloat16)
        .reshape(slots_here, 2, HD)
    )
    keys = keyval[:, 0, :]
    values = keyval[:, 1, :]
    slots = jnp.arange(slots_here, dtype=jnp.int32)
    allowed = (slots[None, :] >= doc_start[:, None]) & (slots[None, :] <= slots[:, None])
    scores = jnp.einsum("peh,kh->epk", query, keys, preferred_element_type=jnp.float32) * scale
    scores = jnp.where(allowed[None], scores, -jnp.inf)
    top = jnp.max(scores, axis=-1, keepdims=True)
    expo = jnp.exp(scores - top)
    probs = expo / jnp.sum(expo, axis=-1, keepdims=True)
    probs_b = probs.astype(jnp.bfloat16)
    attn = jnp.einsum("epk,kh->peh", probs_b, values, preferred_element_type=jnp.float32).astype(
        jnp.bfloat16
    )
    attn = attn.reshape(slots_here, QPK * HD)
    branch_part = jnp.dot(attn, w_out, preferred_element_type=jnp.float32).astype(jnp.bfloat16)
    earlier = from_behind(teacher_hidden[tokens_here - quarter :], "seq", 1)
    features = jnp.concatenate(
        [earlier, teacher_hidden, jnp.zeros((quarter, teacher_hidden.shape[1]), jnp.bfloat16)],
        axis=0,
    )
    picked = lax.dynamic_slice_in_dim(features, start, slots_here, 0)
    projected = jnp.dot(picked, proj_weight, preferred_element_type=jnp.float32).astype(
        jnp.bfloat16
    )
    goal_sum, branch = (
        lax.psum(projected, "tp").astype(jnp.float32),
        lax.psum(branch_part, "tp").astype(jnp.float32),
    )
    goal = goal_sum.astype(jnp.bfloat16)
    student_out = (xf + branch).astype(jnp.bfloat16)
    yf = student_out.astype(jnp.float32)
    tf = goal.astype(jnp.float32)
    live = (slots < count).astype(jnp.float32)[:, None]
    asum = jnp.sum(yf * yf, axis=1, keepdims=True) + epsilon
    bsum = jnp.sum(tf * tf, axis=1, keepdims=True) + epsilon
    both = lax.rsqrt(asum * bsum)
    cosv = jnp.sum(yf * tf, axis=1, keepdims=True) * both
    dy = -math.sqrt(width) * live * (tf * both - cosv * yf / asum)
    dy_b = dy.astype(jnp.bfloat16)
    d_attn = lax.dot_general(
        dy_b, w_out, (((1,), (1,)), ((), ())), preferred_element_type=jnp.float32
    ).astype(jnp.bfloat16)
    d_out = d_attn.reshape(slots_here, QPK, HD)
    d_values = jnp.einsum("epk,peh->kh", probs_b, d_out, preferred_element_type=jnp.float32).astype(
        jnp.bfloat16
    )
    dprob = jnp.einsum("peh,kh->epk", d_out, values, preferred_element_type=jnp.float32)
    dscore = probs * (dprob - jnp.sum(dprob * probs, axis=-1, keepdims=True)) * scale
    dscore_b = dscore.astype(jnp.bfloat16)
    d_query = jnp.einsum("epk,kh->peh", dscore_b, keys, preferred_element_type=jnp.float32).astype(
        jnp.bfloat16
    )
    d_query = d_query.reshape(slots_here, QPK * HD)
    d_keys = jnp.einsum("epk,peh->kh", dscore_b, query, preferred_element_type=jnp.float32).astype(
        jnp.bfloat16
    )
    d_keyval = jnp.stack([d_keys, d_values], axis=1).reshape(slots_here, 2 * HD)
    own_rows = slots_here // lax.axis_size("tp")
    total = lax.dot_general(
        d_query, w_query, (((1,), (1,)), ((), ())), preferred_element_type=jnp.float32
    )
    d_normed = lax.psum_scatter(
        (
            total
            + lax.dot_general(
                d_keyval, w_keyval, (((1,), (1,)), ((), ())), preferred_element_type=jnp.float32
            )
        ).astype(jnp.bfloat16),
        "tp",
        scatter_dimension=0,
        tiled=True,
    ).astype(jnp.float32)
    first_row = lax.axis_index("tp") * own_rows
    x_own = lax.dynamic_slice_in_dim(xf, first_row, own_rows, 0)
    inv_own = lax.dynamic_slice_in_dim(inv, first_row, own_rows, 0)
    dy_own = lax.dynamic_slice_in_dim(dy, first_row, own_rows, 0)
    upper = d_normed * norm_gain
    dx = inv_own * upper - x_own * inv_own * inv_own * inv_own * jnp.mean(
        upper * x_own, axis=1, keepdims=True
    )
    grad_in = (dy_own + dx).astype(jnp.bfloat16)
    return (student_out, grad_in)


MESH = pl.DeviceIdType.MESH


def unrolled(count, step, carry):
    for k in range(count):
        carry = step(k, carry)
    return carry


NT = (((1,), (1,)), ((), ()))
TN = (((0,), (0,)), ((), ()))
F32 = jnp.float32
BF16 = jnp.bfloat16


def dot(a, b, dims=None):
    if dims is None:
        return jnp.dot(a, b, preferred_element_type=F32)
    return lax.dot_general(a, b, dims, preferred_element_type=F32)


def step_kernel(
    n_seq,
    offset_ref,
    count_ref,
    start_hbm,
    gain_hbm,
    teacher_hbm,
    proj_hbm,
    x_hbm,
    wq_hbm,
    wkv_hbm,
    wo_hbm,
    out_ref,
    grad_ref,
    start_s,
    gain_s,
    feat,
    proj,
    x_in,
    wq,
    wkv,
    wo,
    xq,
    normed,
    inv_s,
    qkv,
    probs_s,
    attn_s,
    g_part,
    g_near,
    g_chip,
    g_far,
    b_part,
    b_near,
    b_chip,
    b_far,
    t_s,
    y_s,
    dy_s,
    dy_own,
    d_attn_s,
    dd_s,
    n_part,
    n_near,
    n_chip,
    n_far,
    dn_s,
    load_sem,
    proj_sem,
    send_sem,
    recv_sem,
    shift_sem,
    out_sem,
):
    rows, width = x_in.shape
    quarter = rows // 4
    chunks, _, chunk = proj.shape
    own_tokens = teacher_hbm.shape[0]
    shift = rows - own_tokens
    s = lax.axis_index("seq")
    me = lax.axis_index("tp")
    c = lax.rem(me, 2)
    y = me // 2
    near = {"tp": y * 2 + 1 - c}
    far = {"tp": (1 - y) * 2 + c}
    scale = 1.0 / math.sqrt(HD)

    barrier = pltpu.get_barrier_semaphore()
    pl.semaphore_signal(barrier, inc=1, device_id=near, device_id_type=MESH)
    pl.semaphore_signal(barrier, inc=1, device_id=far, device_id_type=MESH)

    @pl.when(s > 0)
    def _():
        pl.semaphore_signal(barrier, inc=1, device_id={"seq": s - 1}, device_id_type=MESH)

    @pl.when(s < n_seq - 1)
    def _():
        pl.semaphore_signal(barrier, inc=1, device_id={"seq": s + 1}, device_id_type=MESH)

    def gain(k):
        return gain_s[cols(k)][None, :]

    def cols(k):
        if isinstance(k, int):
            return pl.ds(k * chunk, chunk)
        return pl.ds(pl.multiple_of(k * chunk, chunk), chunk)

    loads = [
        pltpu.make_async_copy(a, b, load_sem.at[i])
        for i, (a, b) in enumerate(
            [
                (x_hbm, x_in),
                (wq_hbm, wq),
                (wkv_hbm, wkv),
                (teacher_hbm, feat.at[pl.ds(shift, own_tokens)]),
                (wo_hbm, wo),
                (start_hbm, start_s),
                (gain_hbm, gain_s),
            ]
        )
    ]
    for i in (0, 6, 3, 1):
        loads[i].start()

    def proj_load(k):
        return pltpu.make_async_copy(proj_hbm.at[:, cols(k)], proj.at[k], proj_sem.at[k])

    def start_proj(k, _):
        proj_load(k).start()
        return 0

    lax.fori_loop(0, chunks, start_proj, 0)
    for i in (2, 5, 4):
        loads[i].start()

    loads[0].wait()

    def square(k, acc):
        v = x_in[:, cols(k)].astype(F32)
        for q in range(4):
            xq[q % 2, q // 2, :, cols(k)] = v[q * quarter : (q + 1) * quarter]
        return acc + jnp.sum(v * v, axis=1, keepdims=True)

    total = unrolled(chunks, square, jnp.zeros((rows, 1), F32))
    inv = lax.rsqrt(total / width + epsilon)
    for q in range(4):
        inv_s[q] = inv[q * quarter : (q + 1) * quarter]

    inner = (s > 0) & (s < n_seq - 1)

    @pl.when(inner)
    def _():
        pl.semaphore_wait(barrier, 4)

    @pl.when(jnp.logical_not(inner))
    def _():
        pl.semaphore_wait(barrier, 3)

    def shift_copy(to):
        return pltpu.make_async_remote_copy(
            src_ref=teacher_hbm.at[pl.ds(own_tokens - shift, shift)],
            dst_ref=feat.at[pl.ds(0, shift)],
            send_sem=shift_sem.at[0],
            recv_sem=shift_sem.at[1],
            device_id={"seq": to},
            device_id_type=MESH,
        )

    @pl.when(s < n_seq - 1)
    def _():
        shift_copy(s + 1).start()

    @pl.when(s == 0)
    def _():
        feat[0:shift, :] = jnp.zeros((shift, feat.shape[1]), BF16)

    def remote(kind, k, src, dst, to):
        return pltpu.make_async_remote_copy(
            src_ref=src,
            dst_ref=dst,
            send_sem=send_sem.at[kind, k],
            recv_sem=recv_sem.at[kind, k],
            device_id=to,
            device_id_type=MESH,
        )

    def split_store(ref, k, val):
        for q in range(4):
            ref[k, q % 2, q // 2] = val[q * quarter : (q + 1) * quarter].astype(BF16)

    loads[6].wait()

    def norm(k, _):
        v = x_in[:, cols(k)].astype(F32)
        normed[:, cols(k)] = (v * inv * gain(k)).astype(BF16)
        return 0

    unrolled(chunks, norm, 0)

    loads[1].wait()
    qkv[:, 0 : QPK * HD] = dot(normed[...], wq[...]).astype(BF16)

    start = offset_ref[0] - s * own_tokens + shift
    r_i = lax.broadcasted_iota(jnp.int32, (rows, rows), 0)
    c_i = lax.broadcasted_iota(jnp.int32, (rows, rows), 1)

    @pl.when(s > 0)
    def _():
        shift_copy(s).wait_recv()

    loads[3].wait()
    select = jnp.where(c_i == r_i + start, 1.0, 0.0).astype(BF16)
    feat[...] = dot(select, feat[...]).astype(BF16)

    def near_copy(kind, k, part, land):
        return remote(kind, k, part.at[k, 1 - c], land.at[k], near)

    def far_copy(kind, k, chip, land):
        return remote(kind, k, chip.at[k], land.at[k], far)

    def add_pair(k, part, land, chip):
        pair = part[k, c, 1 - y].astype(F32) + land[k, 1 - y].astype(F32)
        chip[k] = pair.astype(BF16)

    def pass_on(kind, k, part, land, chip, far_land):
        near_copy(kind, k, part, land).wait_recv()
        add_pair(k, part, land, chip)
        far_copy(kind + 1, k, chip, far_land).start()

    def own_sum(kind, k, part, land, chip, far_land):
        far_copy(kind + 1, k, chip, far_land).wait_recv()
        return (
            part[k, c, y].astype(F32) + land[k, y].astype(F32) + far_land[k].astype(F32)
        )

    lag = min(1, chunks)

    def scatter(kind, make, part, land, chip, far_land):
        for k in range(chunks):
            behind = k - lag
            if behind >= 0:
                near_copy(kind, behind, part, land).wait_recv()
            val = make(k)
            if behind >= 0:
                add_pair(behind, part, land, chip)
            split_store(part, k, val)
            near_copy(kind, k, part, land).start()
            if behind >= 0:
                far_copy(kind + 1, behind, chip, far_land).start()

    def scatter_rest(kind, part, land, chip, far_land):
        for k in range(chunks - lag, chunks):
            pass_on(kind, k, part, land, chip, far_land)

    def project(k):
        proj_load(k).wait()
        return dot(feat[...], proj[k])

    goal_bufs = (g_part, g_near, g_chip, g_far)
    scatter(0, project, *goal_bufs)
    loads[2].wait()
    scatter_rest(0, *goal_bufs)
    qkv[:, QPK * HD :] = dot(normed[...], wkv[...]).astype(BF16)
    loads[5].wait()

    starts = jnp.sum(
        jnp.where(r_i == c_i, start_s[...][None, :].astype(F32), 0.0), axis=1, keepdims=True
    )
    c_f = c_i.astype(F32)
    allowed = (c_f >= starts) & (c_i <= r_i)
    keys = qkv[:, QPK * HD : (QPK + 1) * HD]
    values = qkv[:, (QPK + 1) * HD :]
    for e in range(QPK):
        scores = dot(qkv[:, e * HD : (e + 1) * HD], keys, NT) * scale
        scores = jnp.where(allowed, scores, -jnp.inf)
        expo = jnp.exp(scores - jnp.max(scores, axis=-1, keepdims=True))
        probs = expo / jnp.sum(expo, axis=-1, keepdims=True)
        probs_s[e] = probs
        attn_s[:, e * HD : (e + 1) * HD] = dot(probs.astype(BF16), values).astype(BF16)

    loads[4].wait()

    branch_bufs = (b_part, b_near, b_chip, b_far)
    scatter(2, lambda k: dot(attn_s[...], wo[:, cols(k)]), *branch_bufs)
    scatter_rest(2, *branch_bufs)

    def y_copy(kind, k, owner, to):
        return remote(kind, k, y_s.at[k, c, owner], y_s.at[k, c, owner], to)

    def dy_copy(kind, k, owner, to):
        return remote(kind, k, dy_s.at[k, c, owner], dy_s.at[k, c, owner], to)

    def loss_step(k, sums):
        asum, bsum, both = sums
        t = own_sum(0, k, *goal_bufs).astype(BF16).astype(F32)
        t_s[k] = t
        out = (xq[c, y, :, cols(k)] + own_sum(2, k, *branch_bufs)).astype(BF16)
        y_s[k, c, y] = out
        y_copy(5, k, y, near).start()
        out = out.astype(F32)
        return (
            asum + jnp.sum(out * out, axis=-1, keepdims=True),
            bsum + jnp.sum(t * t, axis=-1, keepdims=True),
            both + jnp.sum(out * t, axis=-1, keepdims=True),
        )

    zero = jnp.zeros((quarter, 1), F32)
    asum, bsum, both_sum = unrolled(chunks, loss_step, (zero, zero, zero))
    early = min(3, chunks)

    def start_y(k, _):
        y_copy(4, k, y, far).start()
        return 0

    lax.fori_loop(0, early, start_y, 0)
    asum = asum + epsilon
    bsum = bsum + epsilon
    both = lax.rsqrt(asum * bsum)
    cosv = both_sum * both
    slot = lax.broadcasted_iota(jnp.int32, (quarter, 1), 0) + (2 * y + c) * quarter
    live = jnp.where(slot < count_ref[0], -math.sqrt(width), 0.0)
    t_factor = live * both
    y_factor = live * cosv / asum

    def dy_step(k, _):
        dy = t_s[k] * t_factor - y_s[k, c, y].astype(F32) * y_factor
        dy_s[k, c, y] = dy.astype(BF16)
        dy_copy(7, k, y, far).start()
        dy_copy(8, k, y, near).start()
        dy_own[:, cols(k)] = dy
        return 0

    unrolled(chunks, dy_step, 0)

    d_attn_s[...] = jnp.zeros_like(d_attn_s)

    def d_attn_part(k):
        dy_copy(8, k, y, near).wait_recv()
        dy_copy(9, k, 1 - y, near).wait_recv()
        dy = jnp.concatenate(
            [dy_s[k, q % 2, q // 2].astype(F32) for q in range(4)], axis=0
        ).astype(BF16)
        d_attn_s[...] += dot(dy, wo[:, cols(k)], NT)

    def d_attn_step(k, _):
        dy_copy(7, k, y, far).wait_recv()
        dy_copy(9, k, 1 - y, near).start()

        if k > 0:
            d_attn_part(k - 1)

        return 0

    unrolled(chunks, d_attn_step, 0)
    lax.fori_loop(early, chunks, start_y, 0)
    d_attn_part(chunks - 1)

    d_values = jnp.zeros((rows, HD), F32)
    d_keys = jnp.zeros((rows, HD), F32)
    for e in range(QPK):
        probs = probs_s[e]
        d_out = d_attn_s[:, e * HD : (e + 1) * HD].astype(BF16)
        d_values += dot(probs.astype(BF16), d_out, TN)
        dprob = dot(d_out, values, NT)
        dscore = probs * (dprob - jnp.sum(dprob * probs, axis=-1, keepdims=True)) * scale
        dscore_b = dscore.astype(BF16)
        dd_s[:, e * HD : (e + 1) * HD] = dot(dscore_b, keys).astype(BF16)
        d_keys += dot(dscore_b, qkv[:, e * HD : (e + 1) * HD], TN)
    dd_s[:, QPK * HD : (QPK + 1) * HD] = d_keys.astype(BF16)
    dd_s[:, (QPK + 1) * HD :] = d_values.astype(BF16)

    def d_normed(k):
        return dot(dd_s[:, 0 : QPK * HD], wq[cols(k), :], NT) + dot(
            dd_s[:, QPK * HD :], wkv[cols(k), :], NT
        )

    n_bufs = (n_part, n_near, n_chip, n_far)
    scatter(10, d_normed, *n_bufs)
    scatter_rest(10, *n_bufs)

    def forward_y(k, _):
        y_copy(4, k, y, far).wait_recv()
        y_copy(6, k, 1 - y, near).start()
        return 0

    lax.fori_loop(0, chunks, forward_y, 0)

    def out_copy(k, q):
        return pltpu.make_async_copy(
            y_s.at[k, q % 2, q // 2], out_ref.at[q, :, cols(k)], out_sem.at[k, q]
        )

    def out_step(k, _):
        y_copy(5, k, y, near).wait_recv()
        y_copy(6, k, 1 - y, near).wait_recv()
        for q in range(4):
            out_copy(k, q).start()
        return 0

    lax.fori_loop(0, chunks, out_step, 0)

    def drain_early(k, _):
        for kind, bufs in ((0, goal_bufs), (2, branch_bufs)):
            near_copy(kind, k, bufs[0], bufs[1]).wait_send()
            far_copy(kind + 1, k, bufs[2], bufs[3]).wait_send()
        for first, copy in ((4, y_copy), (7, dy_copy)):
            copy(first, k, y, far).wait_send()
            copy(first + 1, k, y, near).wait_send()
            copy(first + 2, k, 1 - y, near).wait_send()
        return 0

    lax.fori_loop(0, chunks, drain_early, 0)

    @pl.when(s < n_seq - 1)
    def _():
        shift_copy(s + 1).wait_send()

    def sum_step(k, acc):
        upper = own_sum(10, k, *n_bufs) * gain(k)
        dn_s[:, cols(k)] = upper
        return acc + jnp.sum(upper * xq[c, y, :, cols(k)], axis=-1, keepdims=True)

    acc = unrolled(chunks, sum_step, zero)
    inv_own = inv_s[y * 2 + c]
    x_factor = inv_own * inv_own * inv_own * (acc / width)

    def grad_step(k, _):
        dx = inv_own * dn_s[:, cols(k)] - xq[c, y, :, cols(k)] * x_factor
        grad_ref[:, cols(k)] = (dy_own[:, cols(k)] + dx).astype(BF16)
        return 0

    unrolled(chunks, grad_step, 0)

    def drain(k, _):
        for q in range(4):
            out_copy(k, q).wait()
        near_copy(10, k, n_part, n_near).wait_send()
        far_copy(11, k, n_chip, n_far).wait_send()
        return 0

    lax.fori_loop(0, chunks, drain, 0)


def hand_over(y_ref, g_ref, out_ref, grad_ref, y_buf, g_buf, in_sem, out_sem):
    spans = [(y_ref.at[q], y_buf.at[q], out_ref.at[q]) for q in range(4)]
    spans.append((g_ref, g_buf, grad_ref))
    inward = [pltpu.make_async_copy(a, b, in_sem.at[i]) for i, (a, b, _) in enumerate(spans)]
    outward = [pltpu.make_async_copy(b, a, out_sem.at[i]) for i, (_, b, a) in enumerate(spans)]
    for one in inward:
        one.start()
    for one, then in zip(inward, outward):
        one.wait()
        then.start()
    for one in outward:
        one.wait()


def chunk_of(width):
    for size in (512, 256, 128):
        if width % size == 0:
            return size
    return width


def fused_body(
    teacher_hidden,
    proj_weight,
    student_in,
    norm_gain,
    w_query,
    w_keyval,
    w_out,
    row_offsets,
    row_counts,
    doc_start,
):
    rows, width = student_in.shape
    depth = teacher_hidden.shape[1]
    heads = w_query.shape[1]
    quarter = rows // 4
    chunk = chunk_of(width)
    k = width // chunk
    vmem = pltpu.VMEM
    half = (k, 2, quarter, chunk)
    parts = (k, 2, 2, quarter, chunk)
    own = (k, quarter, chunk)
    scratch = [
        vmem((rows,), jnp.int32),
        vmem((width,), F32),
        vmem((rows, depth), BF16),
        vmem((k, depth, chunk), BF16),
        vmem((rows, width), BF16),
        vmem(w_query.shape, BF16),
        vmem(w_keyval.shape, BF16),
        vmem(w_out.shape, BF16),
        vmem((2, 2, quarter, width), F32),
        vmem((rows, width), BF16),
        vmem((4, quarter, 1), F32),
        vmem((rows, 2 * heads), BF16),
        vmem((QPK, rows, rows), F32),
        vmem((rows, heads), BF16),
        vmem(parts, BF16),
        vmem(half, BF16),
        vmem(own, BF16),
        vmem(own, BF16),
        vmem(parts, BF16),
        vmem(half, BF16),
        vmem(own, BF16),
        vmem(own, BF16),
        vmem(own, F32),
        vmem(parts, BF16),
        vmem(parts, BF16),
        vmem((quarter, width), F32),
        vmem((rows, heads), F32),
        vmem((rows, 2 * heads), BF16),
        vmem(parts, BF16),
        vmem(half, BF16),
        vmem(own, BF16),
        vmem(own, BF16),
        vmem((quarter, width), F32),
        pltpu.SemaphoreType.DMA((7,)),
        pltpu.SemaphoreType.DMA((k,)),
        pltpu.SemaphoreType.DMA((12, k)),
        pltpu.SemaphoreType.DMA((12, k)),
        pltpu.SemaphoreType.DMA((2,)),
        pltpu.SemaphoreType.DMA((k, 4)),
    ]
    smem = pl.BlockSpec(memory_space=pltpu.SMEM)
    in_vmem = pl.BlockSpec(memory_space=pltpu.VMEM)
    in_hbm = pl.BlockSpec(memory_space=pltpu.HBM)
    flops = 2 * rows * width * (depth + 6 * heads)
    moved = 2 * width * (depth + 3 * heads + 3 * rows)
    student_out, grad_in = pl.pallas_call(
        functools.partial(step_kernel, lax.axis_size("seq")),
        out_shape=(
            jax.ShapeDtypeStruct((4, quarter, width), BF16),
            jax.ShapeDtypeStruct((quarter, width), BF16),
        ),
        in_specs=[smem, smem] + [in_hbm] * 8,
        out_specs=(in_hbm, in_vmem),
        scratch_shapes=scratch,
        cost_estimate=pl.CostEstimate(flops=flops, bytes_accessed=moved, transcendentals=0),
        compiler_params=pltpu.CompilerParams(
            collective_id=0, has_side_effects=True, vmem_limit_bytes=VMEM_BYTES
        ),
    )(
        row_offsets,
        row_counts,
        doc_start,
        norm_gain,
        teacher_hidden,
        proj_weight,
        student_in,
        w_query,
        w_keyval,
        w_out,
    )
    student_out, grad_in = pl.pallas_call(
        hand_over,
        out_shape=(
            jax.ShapeDtypeStruct(student_out.shape, BF16),
            jax.ShapeDtypeStruct(grad_in.shape, BF16),
        ),
        in_specs=[in_hbm, in_hbm],
        out_specs=(in_hbm, in_hbm),
        scratch_shapes=[
            vmem(student_out.shape, BF16),
            vmem(grad_in.shape, BF16),
            pltpu.SemaphoreType.DMA((5,)),
            pltpu.SemaphoreType.DMA((5,)),
        ],
        compiler_params=pltpu.CompilerParams(vmem_limit_bytes=VMEM_BYTES),
    )(student_out, grad_in)
    return (student_out.reshape(rows, width), grad_in)


VMEM_BYTES = 60 * 2**20


def solution(mesh):
    in_specs = (
        P("seq", "tp"),
        P("tp", None),
        P("seq", None),
        P(),
        P(None, "tp"),
        P(None, "tp"),
        P("tp", None),
        P("seq"),
        P("seq"),
        P("seq"),
    )
    out_specs = (P("seq", None), P(("seq", "tp"), None))
    body = fused_body if mesh.shape["tp"] == 4 else plain_body
    return jax.shard_map(body, mesh=mesh, in_specs=in_specs, out_specs=out_specs, check_vma=False)
```
